32 devices in a mesh: grp: 2 (over x), slab: 16 (over z, y, core).
Axes of the slice: x: 2, y: 2, z: 4, core: 2. Of those that a mesh axis runs over, the one named last changes fastest.
Arguments:
- estimate: float32 [2, 8, 4, 48, 32], P(None, None, 'grp', 'slab'), parts along dimension 2, may hold values from -6 to 6
- measured: float32 [2, 8, 4, 48, 32], P(None, None, 'grp', 'slab'), parts along dimension 2, may hold values from -6 to 6
- sampled_lines: int32 [4, 12], P('grp'), parts along dimension 0, may hold values from 0 to 47, as said below
Outputs:
- updated: float32 [2, 8, 4, 48, 32], P(None, None, 'grp', 'slab'), parts along dimension 2
The draws below stay inside these ranges and needn't reach their ends.
There are 2 independent parts, one for each index of `grp`. The reference program is written for one: setup_inputs(seed, part) draws one part's arguments, and reference() takes and returns one part's arrays. A program takes and returns all parts, laid end to end along the dimension named above; each array names one. Nothing has to cross between parts.
Inputs may be any that keep to these rules, and one draw needn't show every extreme that they name: `sampled_lines`: lines within a frame are distinct, and every frame contains line 48 // 2.
All inputs are finite; a program needn't handle non-finite values.
Results may differ from the reference program's by a relative error of at most 0.0001.
Values sent between devices are 32-bit elements; how exact they have to be, the bound alone decides.
No kernel may reach another device: no remote copies, remote signals or barrier semaphores. Data moves between devices by JAX's collectives and lax.ppermute only.
A program may use at most 64 MiB of HBM per device.

```python
import jax
import jax.numpy as jnp
from jax import lax

C = 8
T_SIZE = 2
KXW = 32
KY_DEV = 3
KY = 48
NS = 12
N_SLAB = 16


def draw_sampled_lines(key, part):
    frames = jnp.arange(T_SIZE, dtype=jnp.int32)

    def one_frame(frame):
        order = jax.random.permutation(jax.random.fold_in(key, frame), KY).astype(jnp.int32)
        centre = KY // 2
        where = jnp.argmax(order == centre)
        order = order.at[where].set(order[0]).at[0].set(centre)
        return order[:NS]
    return jax.vmap(one_frame)(frames).astype(jnp.int32)


def block_scale(stream_key, dims, cuts, smallest, high):
    def one(dim, parts):
        heights = jax.random.uniform(jax.random.fold_in(jax.random.fold_in(stream_key, 6), dim), (parts,), jnp.float32, smallest / len(cuts), high / len(cuts))
        return jnp.repeat(jnp.exp(heights), dims[dim] // parts).reshape((-1,) + (1,) * (len(dims) - dim - 1))

    gain = one(*cuts[0])
    for cut in cuts[1:]:
        gain = gain * one(*cut)
    return gain


def gaussian(rng, dims, spread, reach, cuts=(), held_as=jnp.bfloat16):
    drawn = jax.random.normal(rng, dims, jnp.float32) * spread
    if len(cuts) > 0:
        drawn = block_scale(rng, dims, cuts, -0.22, 0.18) * drawn
    return jnp.clip(drawn, min=-reach, max=reach).astype(held_as)


def setup_inputs(seed: int = 0, part: int = 0) -> dict:
    streams_of = jax.random.split(jax.random.key(seed), 4)
    part_splits = jax.random.split(jax.random.fold_in(streams_of[3], part), 4)
    return {
        "estimate": gaussian(part_splits[0], (2, C, T_SIZE, KY, KXW), 1.0, 6.0, ((3, 16),), jnp.float32),
        "measured": gaussian(part_splits[1], (2, C, T_SIZE, KY, KXW), 1.0, 6.0, ((3, 16),), jnp.float32),
        "sampled_lines": draw_sampled_lines(jax.random.fold_in(jax.random.fold_in(streams_of[3], part), 71), part),
    }


HIGH = lax.Precision.HIGHEST


def build_rows(ext, rows):
    pieces = []
    for shift_t in range(5):
        for shift_y in range(5):
            for shift_x in range(5):
                pieces.append(ext[:, :, shift_t:shift_t + T_SIZE, shift_y:shift_y + rows, shift_x:shift_x + KXW])
    stacked = jnp.stack(pieces, axis=-1)
    stacked = jnp.transpose(stacked, (0, 2, 3, 4, 1, 5))
    return stacked.reshape(2, T_SIZE * rows * KXW, C * 125)


def fold_rows(filtered, rows):
    shaped = filtered.reshape(2, T_SIZE, rows, KXW, C, 125)
    shaped = jnp.transpose(shaped, (0, 4, 1, 2, 3, 5))
    result = jnp.zeros((2, C, T_SIZE + 4, rows + 4, KXW + 4), jnp.float32)
    offset = 0
    for shift_t in range(5):
        for shift_y in range(5):
            for shift_x in range(5):
                result = result.at[:, :, shift_t:shift_t + T_SIZE, shift_y:shift_y + rows, shift_x:shift_x + KXW].add(shaped[..., offset])
                offset += 1
    return result / 125.0


def reference(estimate, measured, sampled_lines):
    padded = jnp.pad(estimate, ((0, 0), (0, 0), (2, 2), (2, 2), (2, 2)))
    width = 125 * C
    starts = jnp.arange(N_SLAB, dtype=jnp.int32) * KY_DEV

    def gram_step(carry, start):
        ext = lax.dynamic_slice_in_dim(padded, start, KY_DEV + 4, 3)
        patch = build_rows(ext, KY_DEV)
        real_part, imag_part = patch[0], patch[1]
        real_gram = jnp.dot(real_part.T, real_part, precision=HIGH) + jnp.dot(imag_part.T, imag_part, precision=HIGH)
        imag_gram = jnp.dot(real_part.T, imag_part, precision=HIGH) - jnp.dot(imag_part.T, real_part, precision=HIGH)
        return (carry[0] + real_gram, carry[1] + imag_gram), None

    zeros = jnp.zeros((width, width), jnp.float32)
    (real_gram, imag_gram), unused = lax.scan(gram_step, (zeros, zeros), starts)
    scale = jnp.trace(real_gram) / width + 1e-6
    real_gram = real_gram / scale
    imag_gram = imag_gram / scale

    def fold_step(total, start):
        ext = lax.dynamic_slice_in_dim(padded, start, KY_DEV + 4, 3)
        patch = build_rows(ext, KY_DEV)
        real_part, imag_part = patch[0], patch[1]
        real_out = jnp.dot(real_part, real_gram, precision=HIGH) - jnp.dot(imag_part, imag_gram, precision=HIGH)
        imag_out = jnp.dot(real_part, imag_gram, precision=HIGH) + jnp.dot(imag_part, real_gram, precision=HIGH)
        piece = fold_rows(jnp.stack([real_out, imag_out]), KY_DEV)
        current = lax.dynamic_slice_in_dim(total, start, KY_DEV + 4, 3)
        total = lax.dynamic_update_slice_in_dim(total, current + piece, start, 3)
        return total, None

    total = jnp.zeros((2, C, T_SIZE + 4, KY + 4, KXW + 4), jnp.float32)
    total, unused = lax.scan(fold_step, total, starts)
    folded = total[:, :, 2:-2, 2:-2, 2:-2]
    rows = jnp.arange(KY, dtype=jnp.int32)
    hit = jnp.any(sampled_lines[:, :, None] == rows[None, None, :], axis=1)
    weight = hit.astype(jnp.float32)[None, None, :, :, None]
    return weight * measured + (1.0 - weight) * folded
```

```python
import functools

import jax
import jax.numpy as jnp
from jax import lax
from jax.experimental import pallas as pl
from jax.experimental.pallas import tpu as pltpu
from jax.sharding import PartitionSpec as P

SPAN = 5
HALF = SPAN // 2
LAGS = SPAN - 1
LANES = 128
NT = (((1,), (1,)), ((), ()))
NN = (((1,), (0,)), ((), ()))


def up(size, unit):
    return -(-size // unit) * unit


def split(value):
    high = value.astype(jnp.bfloat16)
    return high, (value - high.astype(jnp.float32)).astype(jnp.bfloat16)


def repeat(count, body):
    if count <= 16:
        for step in range(count):
            body(step)
    else:
        lax.fori_loop(0, count, lambda step, carry: (body(step), carry)[1], 0)


def lane_tile(tile):
    start = tile * LANES
    return start if isinstance(start, int) else pl.multiple_of(start, LANES)


def kernel(sizes, lines_ref, gathered_ref, measured_ref, out_ref, x_ref, z_ref, zc_ref, acc_ref, xw_ref, lhs_ref, rhs_ref):
    slabs, coils, frames, rows, readout, samples = sizes
    me = lax.axis_index("slab")
    cell = coils * frames
    band = SPAN * cell
    width = rows * readout
    groups = LANES // readout
    lines = slabs * rows
    tiles = up(lines, groups) // groups
    f32 = jnp.float32

    if tiles * groups != lines:
        x_ref[...] = jnp.zeros_like(x_ref)
    for line in range(lines):
        block, inner = divmod(line, rows)
        group, tile = divmod(line, tiles)
        start = (LAGS + tile) * LANES + group * readout
        x_ref[:, start : start + readout] = gathered_ref[block, :, inner * readout : (inner + 1) * readout]
    lane = lax.broadcasted_iota(jnp.int32, (2 * cell, LANES), 1)
    for back in range(1, LAGS + 1):
        source = (LAGS + tiles - back) * LANES
        wrapped = pltpu.roll(x_ref[:, source : source + LANES], readout, 1)
        target = (LAGS - back) * LANES
        x_ref[:, target : target + LANES] = jnp.where(lane >= readout, wrapped, 0.0)

    column = lane % readout
    inside = [(column + e - HALF >= 0) & (column + e - HALF < readout) for e in range(SPAN)]

    def patches(tile):
        at = pl.ds(lane_tile(tile), LANES)
        cells = x_ref[:, at]
        for e in range(SPAN):
            moved = cells if e == HALF else pltpu.roll(cells, (HALF - e) % LANES, 1)
            high, low = split(jnp.where(inside[e], moved, 0.0))
            for part in range(2):
                first = part * band + e * cell
                z_ref[first : first + cell, at] = high[part * cell : (part + 1) * cell]
                z_ref[2 * band + first : 2 * band + first + cell, at] = low[part * cell : (part + 1) * cell]

    repeat(LAGS + tiles, patches)

    pad = up(band, LANES)

    def centre(tile):
        source = pl.ds(lane_tile(tile + LAGS), LANES)
        at = pl.ds(lane_tile(tile), LANES)
        for piece in range(4):
            first = piece * pad
            zc_ref[first : first + band, at] = z_ref[piece * band : (piece + 1) * band, source]
            zc_ref[first + band : first + pad, at] = jnp.zeros((pad - band, LANES), jnp.bfloat16)

    repeat(tiles, centre)

    line_base = lane // readout * tiles
    acc_ref[...] = jnp.zeros_like(acc_ref)

    def energy(tile):
        cells = x_ref[:, pl.ds(lane_tile(tile + LAGS), LANES)]
        line = line_base + tile
        covers = jnp.minimum(line + HALF, lines - 1) - jnp.maximum(line - HALF, 0) + 1
        acc_ref[...] += cells * cells * covers.astype(f32)

    repeat(tiles, energy)
    row = lax.broadcasted_iota(jnp.int32, (2 * cell, LANES), 0)
    frame = row // coils % frames
    covers_t = jnp.minimum(frame + HALF, frames - 1) - jnp.maximum(frame - HALF, 0) + 1
    covers_x = jnp.minimum(column + HALF, readout - 1) - jnp.maximum(column - HALF, 0) + 1
    weighted = acc_ref[...] * (covers_t * covers_x).astype(f32)
    trace = jnp.sum(jnp.sum(weighted, axis=1, keepdims=True), axis=0, keepdims=True)
    scale = trace / (SPAN**3 * coils) + 1e-06

    def product(left, right):
        both = lax.dot_general(left, right[: 2 * pad], NT, preferred_element_type=f32)
        cross = lax.dot_general(left[: 2 * band], right[2 * pad :], NT, preferred_element_type=f32)
        return both[: 2 * band] + both[2 * band :] + cross

    mrow = lax.broadcasted_iota(jnp.int32, (band, pad), 0) // coils % frames
    mcol = lax.broadcasted_iota(jnp.int32, (band, pad), 1) // coils % frames
    mixes = []
    for shift in range(-frames + 1, frames):
        mask = jnp.zeros((band, pad), f32)
        for i in range(frames):
            for j in range(frames):
                if 0 <= i + shift < frames and 0 <= j + shift < frames:
                    count = sum(
                        abs(i - t) <= HALF and abs(j - t) <= HALF and 0 <= t + shift < frames for t in range(frames)
                    )
                    mask = jnp.where((mrow == i) & (mcol == j), float(count), mask)
        mixes.append((shift, mask))

    def mixed(gram):
        total = None
        for shift, mask in mixes:
            moved = gram
            if shift:
                moved = pltpu.roll(pltpu.roll(gram, -shift * coils % pad, 1), -shift * coils % band, 0)
            total = moved * mask if total is None else total + moved * mask
        return total

    def complex_gram(stacked):
        real = stacked[:band, :pad] + stacked[band:, pad:]
        imag = stacked[:band, pad:] - stacked[band:, :pad]
        return mixed(real), mixed(imag)

    slot = 0
    order = []

    def put(real, imag, lag, weight):
        nonlocal slot
        lhs_ref[:band, slot * pad : (slot + 1) * pad] = real
        lhs_ref[band:, slot * pad : (slot + 1) * pad] = imag
        order.append((lag, weight))
        slot += 1

    def put_both(pair, lag, weight, back_weight):
        real, imag = pair
        put(real, imag, lag, weight)
        fill = jnp.zeros((pad - band, pad), f32)
        real_t = jnp.transpose(jnp.concatenate([real, fill], axis=0))[:band]
        imag_t = jnp.transpose(jnp.concatenate([imag, fill], axis=0))[:band]
        put(real_t, -imag_t, -lag, back_weight)

    window = lax.broadcasted_iota(jnp.int32, (cell, up(width, LANES)), 1)
    my_line = me * rows + window // readout
    valid = [((my_line - b + HALF >= 0) & (my_line - b + HALF < lines)).astype(f32) for b in range(SPAN)]

    def lag_weight(lag):
        total = None
        for b in range(SPAN):
            if 0 <= b + lag < SPAN:
                total = valid[b] if total is None else total + valid[b]
        return total

    depth = max(d for d in range(1, 17) if tiles % d == 0)
    for lag in range(SPAN):

        def part(step):
            left = z_ref[:, pl.ds(lane_tile(LAGS - lag + step * depth), depth * LANES)]
            right = zc_ref[:, pl.ds(lane_tile(step * depth), depth * LANES)]
            return product(left, right)

        if tiles == depth:
            stacked = part(0)
        else:
            stacked = lax.fori_loop(
                0, tiles // depth, lambda step, total: total + part(step), jnp.zeros((2 * band, 2 * pad), f32)
            )
        pair = complex_gram(stacked)
        if lag == 0:
            put(*pair, 0, lag_weight(0))
        else:
            put_both(pair, lag, lag_weight(lag), lag_weight(-lag))

    def edge(first, second):
        group, tile = divmod(first, tiles)
        other = second % tiles
        start = (LAGS + tile) * LANES
        here = lax.broadcasted_iota(jnp.int32, (4 * band, LANES), 1) // readout == group
        left = jnp.where(here, z_ref[:, start : start + LANES].astype(f32), 0.0).astype(jnp.bfloat16)
        return complex_gram(product(left, zc_ref[:, other * LANES : (other + 1) * LANES]))

    last = lines - 1
    put(*edge(last - 1, last - 1), 0, -valid[0])
    put(*edge(last, last), 0, -(valid[0] + valid[1]))
    put(*edge(0, 0), 0, -(valid[3] + valid[4]))
    put(*edge(1, 1), 0, -valid[4])
    put_both(edge(last - 1, last), 1, -valid[0], -valid[1])
    put_both(edge(0, 1), 1, -valid[3], -valid[4])

    reach = up(LAGS, rows) // rows
    for j in range(-reach, reach + 1):
        block = me + j
        held = gathered_ref[jnp.clip(block, 0, slabs - 1)]
        held = jnp.where((block >= 0) & (block < slabs), held, 0.0)
        xw_ref[:, (j + reach) * width : (j + reach + 1) * width] = held
    extent = xw_ref.shape[1]
    spread = lax.broadcasted_iota(jnp.int32, (2 * cell, extent), 1) % readout
    around = xw_ref[...]
    wide = up(width, LANES)
    for e in range(SPAN):
        moved = around if e == HALF else pltpu.roll(around, (HALF - e) % extent, 1)
        near = spread + e - HALF
        moved = jnp.where((near >= 0) & (near < readout), moved, 0.0)
        for lag in range(-LAGS, LAGS + 1):
            start = (reach * rows + lag) * readout
            piece = moved[:, start : start + wide]
            for index, (at, weight) in enumerate(order):
                if at == lag:
                    first = index * pad + e * cell
                    for part in range(2):
                        high, low = split(piece[part * cell : (part + 1) * cell] * weight)
                        rhs_ref[first : first + cell, part * wide : (part + 1) * wide] = high
                        rhs_ref[first : first + cell, (2 + part) * wide : (3 + part) * wide] = low
    for index in range(len(order)):
        first = index * pad
        rhs_ref[first + band : first + pad, :] = jnp.zeros((pad - band, 4 * wide), jnp.bfloat16)

    high, low = split(lhs_ref[...])
    lead = rhs_ref[:, : 2 * wide]
    total = lax.dot_general(high, lead, NN, preferred_element_type=f32)
    total += lax.dot_general(low, lead, NN, preferred_element_type=f32)
    total += lax.dot_general(high, rhs_ref[:, 2 * wide :], NN, preferred_element_type=f32)
    real = total[:band, :wide] + total[band:, wide:]
    imag = total[:band, wide:] - total[band:, :wide]

    factor = 1.0 / (SPAN**3 * scale)
    column = window % readout
    frame = lax.broadcasted_iota(jnp.int32, (cell, wide), 0) // coils
    hit = jnp.zeros((cell, wide), jnp.int32)
    for f in range(frames):
        for sample in range(samples):
            same = (my_line == lines_ref[f, sample]) & (frame == f)
            hit = jnp.where(same, 1, hit)
    for part, values in enumerate((real, imag)):
        folded = jnp.zeros((cell, wide), f32)
        for e in range(SPAN):
            moved = values[e * cell : (e + 1) * cell]
            if e != HALF:
                moved = pltpu.roll(moved, (e - HALF) % wide, 1)
            near = column - e + HALF
            folded += jnp.where((near >= 0) & (near < readout), moved, 0.0)
        folded = (folded * factor)[:, :width]
        kept = measured_ref[part * cell : (part + 1) * cell, :]
        out_ref[part * cell : (part + 1) * cell, :] = jnp.where(hit[:, :width] > 0, kept, folded)


def gather(block):
    return lax.all_gather(block, "slab")


def local(estimate, measured, sampled_lines):
    _, coils, frames, rows, readout = estimate.shape
    slabs = lax.axis_size("slab")
    cell = coils * frames
    width = rows * readout
    band = SPAN * cell
    pad = up(band, LANES)
    wide = up(width, LANES)
    groups = LANES // readout
    tiles = up(slabs * rows, groups) // groups
    reach = up(LAGS, rows) // rows
    slots = 2 * SPAN - 1 + 8

    def flat(array):
        return jnp.swapaxes(array, 1, 2).reshape(2 * cell, width)

    gathered = gather(flat(estimate))
    sizes = (slabs, coils, frames, rows, readout, sampled_lines.shape[1])
    vmem = pl.BlockSpec(memory_space=pltpu.VMEM)
    result = pl.pallas_call(
        functools.partial(kernel, sizes),
        out_shape=jax.ShapeDtypeStruct((2 * cell, width), jnp.float32),
        in_specs=[pl.BlockSpec(memory_space=pltpu.SMEM), vmem, vmem],
        out_specs=vmem,
        scratch_shapes=[
            pltpu.VMEM((2 * cell, (LAGS + tiles) * LANES), jnp.float32),
            pltpu.VMEM((4 * band, (LAGS + tiles) * LANES), jnp.bfloat16),
            pltpu.VMEM((4 * pad, tiles * LANES), jnp.bfloat16),
            pltpu.VMEM((2 * cell, LANES), jnp.float32),
            pltpu.VMEM((2 * cell, up((2 * reach + 1) * width + LANES, LANES)), jnp.float32),
            pltpu.VMEM((2 * band, slots * pad), jnp.float32),
            pltpu.VMEM((slots * pad, 4 * wide), jnp.bfloat16),
        ],
        compiler_params=pltpu.CompilerParams(vmem_limit_bytes=48 * 1024 * 1024),
        name="filter_step",
    )(sampled_lines, gathered, flat(measured))
    return jnp.swapaxes(result.reshape(2, frames, coils, rows, readout), 1, 2)


def solution(mesh):
    placed = (
        P(None, None, "grp", "slab", None),
        P(None, None, "grp", "slab", None),
        P("grp", None),
    )
    return jax.shard_map(
        local,
        mesh=mesh,
        in_specs=placed,
        out_specs=P(None, None, "grp", "slab", None),
        check_vma=False,
    )
```

```python
import functools

import jax
import jax.numpy as jnp
from jax import lax
from jax.experimental import pallas as pl
from jax.experimental.pallas import tpu as pltpu
from jax.sharding import PartitionSpec as P

SPAN = 5
HALF = SPAN // 2
LAGS = SPAN - 1
LANES = 128
NT = (((1,), (1,)), ((), ()))
NN = (((1,), (0,)), ((), ()))


def up(size, unit):
    return -(-size // unit) * unit


def split(value):
    high = value.astype(jnp.bfloat16)
    return high, (value - high.astype(jnp.float32)).astype(jnp.bfloat16)


def repeat(count, body):
    if count <= 16:
        for step in range(count):
            body(step)
    else:
        lax.fori_loop(0, count, lambda step, carry: (body(step), carry)[1], 0)


def lane_tile(tile):
    start = tile * LANES
    return start if isinstance(start, int) else pl.multiple_of(start, LANES)


def kernel(sizes, lines_ref, gathered_ref, measured_ref, out_ref, x_ref, z_ref, zc_ref, acc_ref, xw_ref, lhs_ref, rhs_ref):
    slabs, coils, frames, rows, readout, samples = sizes
    me = lax.axis_index("slab")
    cell = coils * frames
    band = SPAN * cell
    width = rows * readout
    groups = LANES // readout
    lines = slabs * rows
    tiles = up(lines, groups) // groups
    f32 = jnp.float32

    if tiles * groups != lines:
        x_ref[...] = jnp.zeros_like(x_ref)
    for line in range(lines):
        block, inner = divmod(line, rows)
        group, tile = divmod(line, tiles)
        start = (LAGS + tile) * LANES + group * readout
        x_ref[:, start : start + readout] = gathered_ref[block, :, inner * readout : (inner + 1) * readout]
    lane = lax.broadcasted_iota(jnp.int32, (2 * cell, LANES), 1)
    for back in range(1, LAGS + 1):
        source = (LAGS + tiles - back) * LANES
        wrapped = pltpu.roll(x_ref[:, source : source + LANES], readout, 1)
        target = (LAGS - back) * LANES
        x_ref[:, target : target + LANES] = jnp.where(lane >= readout, wrapped, 0.0)

    column = lane % readout
    inside = [(column + e - HALF >= 0) & (column + e - HALF < readout) for e in range(SPAN)]

    def patches(tile):
        at = pl.ds(lane_tile(tile), LANES)
        cells = x_ref[:, at]
        for e in range(SPAN):
            moved = cells if e == HALF else pltpu.roll(cells, (HALF - e) % LANES, 1)
            high, low = split(jnp.where(inside[e], moved, 0.0))
            for part in range(2):
                first = part * band + e * cell
                z_ref[first : first + cell, at] = high[part * cell : (part + 1) * cell]
                z_ref[2 * band + first : 2 * band + first + cell, at] = low[part * cell : (part + 1) * cell]

    repeat(LAGS + tiles, patches)

    pad = up(band, LANES)

    def centre(tile):
        source = pl.ds(lane_tile(tile + LAGS), LANES)
        at = pl.ds(lane_tile(tile), LANES)
        for piece in range(4):
            first = piece * pad
            zc_ref[first : first + band, at] = z_ref[piece * band : (piece + 1) * band, source]
            zc_ref[first + band : first + pad, at] = jnp.zeros((pad - band, LANES), jnp.bfloat16)

    repeat(tiles, centre)

    line_base = lane // readout * tiles
    acc_ref[...] = jnp.zeros_like(acc_ref)

    def energy(tile):
        cells = x_ref[:, pl.ds(lane_tile(tile + LAGS), LANES)]
        line = line_base + tile
        covers = jnp.minimum(line + HALF, lines - 1) - jnp.maximum(line - HALF, 0) + 1
        acc_ref[...] += cells * cells * covers.astype(f32)

    repeat(tiles, energy)
    row = lax.broadcasted_iota(jnp.int32, (2 * cell, LANES), 0)
    frame = row // coils % frames
    covers_t = jnp.minimum(frame + HALF, frames - 1) - jnp.maximum(frame - HALF, 0) + 1
    covers_x = jnp.minimum(column + HALF, readout - 1) - jnp.maximum(column - HALF, 0) + 1
    weighted = acc_ref[...] * (covers_t * covers_x).astype(f32)
    trace = jnp.sum(jnp.sum(weighted, axis=1, keepdims=True), axis=0, keepdims=True)
    scale = trace / (SPAN**3 * coils) + 1e-06

    def product(left, right):
        both = lax.dot_general(left, right[: 2 * pad], NT, preferred_element_type=f32)
        cross = lax.dot_general(left[: 2 * band], right[2 * pad :], NT, preferred_element_type=f32)
        return both[: 2 * band] + both[2 * band :] + cross

    mrow = lax.broadcasted_iota(jnp.int32, (band, pad), 0) // coils % frames
    mcol = lax.broadcasted_iota(jnp.int32, (band, pad), 1) // coils % frames
    mixes = []
    for shift in range(-frames + 1, frames):
        mask = jnp.zeros((band, pad), f32)
        for i in range(frames):
            for j in range(frames):
                if 0 <= i + shift < frames and 0 <= j + shift < frames:
                    count = sum(
                        abs(i - t) <= HALF and abs(j - t) <= HALF and 0 <= t + shift < frames for t in range(frames)
                    )
                    mask = jnp.where((mrow == i) & (mcol == j), float(count), mask)
        mixes.append((shift, mask))

    def mixed(gram):
        total = None
        for shift, mask in mixes:
            moved = gram
            if shift:
                moved = pltpu.roll(pltpu.roll(gram, -shift * coils % pad, 1), -shift * coils % band, 0)
            total = moved * mask if total is None else total + moved * mask
        return total

    def complex_gram(stacked):
        real = stacked[:band, :pad] + stacked[band:, pad:]
        imag = stacked[:band, pad:] - stacked[band:, :pad]
        return mixed(real), mixed(imag)

    slot = 0
    order = []

    def put(real, imag, lag, weight):
        nonlocal slot
        lhs_ref[:band, slot * pad : (slot + 1) * pad] = real
        lhs_ref[band:, slot * pad : (slot + 1) * pad] = imag
        order.append((lag, weight))
        slot += 1

    def put_both(pair, lag, weight, back_weight):
        real, imag = pair
        put(real, imag, lag, weight)
        fill = jnp.zeros((pad - band, pad), f32)
        real_t = jnp.transpose(jnp.concatenate([real, fill], axis=0))[:band]
        imag_t = jnp.transpose(jnp.concatenate([imag, fill], axis=0))[:band]
        put(real_t, -imag_t, -lag, back_weight)

    window = lax.broadcasted_iota(jnp.int32, (cell, up(width, LANES)), 1)
    my_line = me * rows + window // readout
    valid = [((my_line - b + HALF >= 0) & (my_line - b + HALF < lines)).astype(f32) for b in range(SPAN)]

    def lag_weight(lag):
        total = None
        for b in range(SPAN):
            if 0 <= b + lag < SPAN:
                total = valid[b] if total is None else total + valid[b]
        return total

    depth = max(d for d in range(1, 17) if tiles % d == 0)
    for lag in range(SPAN):

        def part(step):
            left = z_ref[:, pl.ds(lane_tile(LAGS - lag + step * depth), depth * LANES)]
            right = zc_ref[:, pl.ds(lane_tile(step * depth), depth * LANES)]
            return product(left, right)

        if tiles == depth:
            stacked = part(0)
        else:
            stacked = lax.fori_loop(
                0, tiles // depth, lambda step, total: total + part(step), jnp.zeros((2 * band, 2 * pad), f32)
            )
        pair = complex_gram(stacked)
        if lag == 0:
            put(*pair, 0, lag_weight(0))
        else:
            put_both(pair, lag, lag_weight(lag), lag_weight(-lag))

    def edge(first, second):
        group, tile = divmod(first, tiles)
        other = second % tiles
        start = (LAGS + tile) * LANES
        here = lax.broadcasted_iota(jnp.int32, (4 * band, LANES), 1) // readout == group
        left = jnp.where(here, z_ref[:, start : start + LANES].astype(f32), 0.0).astype(jnp.bfloat16)
        return complex_gram(product(left, zc_ref[:, other * LANES : (other + 1) * LANES]))

    last = lines - 1
    put(*edge(last - 1, last - 1), 0, -valid[0])
    put(*edge(last, last), 0, -(valid[0] + valid[1]))
    put(*edge(0, 0), 0, -(valid[3] + valid[4]))
    put(*edge(1, 1), 0, -valid[4])
    put_both(edge(last - 1, last), 1, -valid[0], -valid[1])
    put_both(edge(0, 1), 1, -valid[3], -valid[4])

    reach = up(LAGS, rows) // rows
    for j in range(-reach, reach + 1):
        block = me + j
        held = gathered_ref[jnp.clip(block, 0, slabs - 1)]
        held = jnp.where((block >= 0) & (block < slabs), held, 0.0)
        xw_ref[:, (j + reach) * width : (j + reach + 1) * width] = held
    extent = xw_ref.shape[1]
    spread = lax.broadcasted_iota(jnp.int32, (2 * cell, extent), 1) % readout
    around = xw_ref[...]
    wide = up(width, LANES)
    for e in range(SPAN):
        moved = around if e == HALF else pltpu.roll(around, (HALF - e) % extent, 1)
        near = spread + e - HALF
        moved = jnp.where((near >= 0) & (near < readout), moved, 0.0)
        for lag in range(-LAGS, LAGS + 1):
            start = (reach * rows + lag) * readout
            piece = moved[:, start : start + wide]
            for index, (at, weight) in enumerate(order):
                if at == lag:
                    first = index * pad + e * cell
                    for part in range(2):
                        high, low = split(piece[part * cell : (part + 1) * cell] * weight)
                        rhs_ref[first : first + cell, part * wide : (part + 1) * wide] = high
                        rhs_ref[first : first + cell, (2 + part) * wide : (3 + part) * wide] = low
    for index in range(len(order)):
        first = index * pad
        rhs_ref[first + band : first + pad, :] = jnp.zeros((pad - band, 4 * wide), jnp.bfloat16)

    high, low = split(lhs_ref[...])
    lead = rhs_ref[:, : 2 * wide]
    total = lax.dot_general(high, lead, NN, preferred_element_type=f32)
    total += lax.dot_general(low, lead, NN, preferred_element_type=f32)
    total += lax.dot_general(high, rhs_ref[:, 2 * wide :], NN, preferred_element_type=f32)
    real = total[:band, :wide] + total[band:, wide:]
    imag = total[:band, wide:] - total[band:, :wide]

    factor = 1.0 / (SPAN**3 * scale)
    column = window % readout
    hits = {}
    for line in range(rows):
        for f in range(frames):
            hit = lines_ref[f, 0] == me * rows + line
            for sample in range(1, samples):
                hit |= lines_ref[f, sample] == me * rows + line
            hits[line, f] = hit
    for part, values in enumerate((real, imag)):
        folded = jnp.zeros((cell, wide), f32)
        for e in range(SPAN):
            moved = values[e * cell : (e + 1) * cell]
            if e != HALF:
                moved = pltpu.roll(moved, (e - HALF) % wide, 1)
            near = column - e + HALF
            folded += jnp.where((near >= 0) & (near < readout), moved, 0.0)
        folded = folded * factor
        for line in range(rows):
            for f in range(frames):
                kept = measured_ref[part, :, line, f, :]
                mine = folded[f * coils : (f + 1) * coils, line * readout : (line + 1) * readout]
                out_ref[part, :, line, f, :] = jnp.where(hits[line, f], kept, mine)


def gather(block):
    copies = jnp.broadcast_to(block[None], (lax.axis_size("slab"),) + block.shape)
    return lax.all_to_all(copies, "slab", 0, 0)


def local(estimate, measured, sampled_lines):
    _, coils, frames, rows, readout = estimate.shape
    slabs = lax.axis_size("slab")
    cell = coils * frames
    width = rows * readout
    band = SPAN * cell
    pad = up(band, LANES)
    wide = up(width, LANES)
    groups = LANES // readout
    tiles = up(slabs * rows, groups) // groups
    reach = up(LAGS, rows) // rows
    slots = 2 * SPAN - 1 + 8

    def flat(array):
        return jnp.swapaxes(array, 1, 2).reshape(2 * cell, width)

    gathered = gather(flat(estimate))
    sizes = (slabs, coils, frames, rows, readout, sampled_lines.shape[1])
    vmem = pl.BlockSpec(memory_space=pltpu.VMEM)
    result = pl.pallas_call(
        functools.partial(kernel, sizes),
        out_shape=jax.ShapeDtypeStruct((2, coils, rows, frames, readout), jnp.float32),
        in_specs=[pl.BlockSpec(memory_space=pltpu.SMEM), vmem, vmem],
        out_specs=vmem,
        scratch_shapes=[
            pltpu.VMEM((2 * cell, (LAGS + tiles) * LANES), jnp.float32),
            pltpu.VMEM((4 * band, (LAGS + tiles) * LANES), jnp.bfloat16),
            pltpu.VMEM((4 * pad, tiles * LANES), jnp.bfloat16),
            pltpu.VMEM((2 * cell, LANES), jnp.float32),
            pltpu.VMEM((2 * cell, up((2 * reach + 1) * width + LANES, LANES)), jnp.float32),
            pltpu.VMEM((2 * band, slots * pad), jnp.float32),
            pltpu.VMEM((slots * pad, 4 * wide), jnp.bfloat16),
        ],
        compiler_params=pltpu.CompilerParams(vmem_limit_bytes=48 * 1024 * 1024),
        name="filter_step",
    )(sampled_lines, gathered, jnp.swapaxes(measured, 2, 3))
    return jnp.swapaxes(result, 2, 3)


def solution(mesh):
    placed = (
        P(None, None, "grp", "slab", None),
        P(None, None, "grp", "slab", None),
        P("grp", None),
    )
    return jax.shard_map(
        local,
        mesh=mesh,
        in_specs=placed,
        out_specs=P(None, None, "grp", "slab", None),
        check_vma=False,
    )
```

```python
import functools

import jax
import jax.numpy as jnp
from jax import lax
from jax.experimental import pallas as pl
from jax.experimental.pallas import tpu as pltpu
from jax.sharding import PartitionSpec as P

SPAN = 5
HALF = SPAN // 2
LAGS = SPAN - 1
LANES = 128
NT = (((1,), (1,)), ((), ()))
NN = (((1,), (0,)), ((), ()))


def up(size, unit):
    return -(-size // unit) * unit


def split(value):
    high = value.astype(jnp.bfloat16)
    return high, (value - high.astype(jnp.float32)).astype(jnp.bfloat16)


def repeat(count, body):
    if count <= 16:
        for step in range(count):
            body(step)
    else:
        lax.fori_loop(0, count, lambda step, carry: (body(step), carry)[1], 0)


def lane_tile(tile):
    start = tile * LANES
    return start if isinstance(start, int) else pl.multiple_of(start, LANES)


def kernel(sizes, hit_ref, gathered_ref, measured_ref, out_ref, x_ref, z_ref, zc_ref, acc_ref, xw_ref, lhs_ref, rhs_ref):
    slabs, coils, frames, rows, readout = sizes
    me = lax.axis_index("slab")
    cell = coils * frames
    band = SPAN * cell
    width = rows * readout
    groups = LANES // readout
    lines = slabs * rows
    tiles = up(lines, groups) // groups
    f32 = jnp.float32

    planes = 2 * frames

    def unpacked(block, plane, line):
        down, right = divmod(plane * rows + line, groups)
        near = nearby(slabs)
        place = block % near * (slabs // near) + block // near
        return gathered_ref[place, down * coils : (down + 1) * coils, right * readout : (right + 1) * readout]

    if tiles * groups != lines:
        x_ref[...] = jnp.zeros_like(x_ref)
    for line in range(lines):
        block, inner = divmod(line, rows)
        group, tile = divmod(line, tiles)
        start = (LAGS + tile) * LANES + group * readout
        for plane in range(planes):
            x_ref[plane * coils : (plane + 1) * coils, start : start + readout] = unpacked(block, plane, inner)
    lane = lax.broadcasted_iota(jnp.int32, (2 * cell, LANES), 1)
    for back in range(1, LAGS + 1):
        source = (LAGS + tiles - back) * LANES
        wrapped = pltpu.roll(x_ref[:, source : source + LANES], readout, 1)
        target = (LAGS - back) * LANES
        x_ref[:, target : target + LANES] = jnp.where(lane >= readout, wrapped, 0.0)

    column = lane % readout
    inside = [(column + e - HALF >= 0) & (column + e - HALF < readout) for e in range(SPAN)]

    def patches(tile):
        at = pl.ds(lane_tile(tile), LANES)
        cells = x_ref[:, at]
        for e in range(SPAN):
            moved = cells if e == HALF else pltpu.roll(cells, (HALF - e) % LANES, 1)
            high, low = split(jnp.where(inside[e], moved, 0.0))
            for part in range(2):
                first = part * band + e * cell
                z_ref[first : first + cell, at] = high[part * cell : (part + 1) * cell]
                z_ref[2 * band + first : 2 * band + first + cell, at] = low[part * cell : (part + 1) * cell]

    repeat(LAGS + tiles, patches)

    pad = up(band, LANES)

    def centre(tile):
        source = pl.ds(lane_tile(tile + LAGS), LANES)
        at = pl.ds(lane_tile(tile), LANES)
        for piece in range(4):
            first = piece * pad
            zc_ref[first : first + band, at] = z_ref[piece * band : (piece + 1) * band, source]
            zc_ref[first + band : first + pad, at] = jnp.zeros((pad - band, LANES), jnp.bfloat16)

    repeat(tiles, centre)

    line_base = lane // readout * tiles
    acc_ref[...] = jnp.zeros_like(acc_ref)

    def energy(tile):
        cells = x_ref[:, pl.ds(lane_tile(tile + LAGS), LANES)]
        line = line_base + tile
        covers = jnp.minimum(line + HALF, lines - 1) - jnp.maximum(line - HALF, 0) + 1
        acc_ref[...] += cells * cells * covers.astype(f32)

    repeat(tiles, energy)
    row = lax.broadcasted_iota(jnp.int32, (2 * cell, LANES), 0)
    frame = row // coils % frames
    covers_t = jnp.minimum(frame + HALF, frames - 1) - jnp.maximum(frame - HALF, 0) + 1
    covers_x = jnp.minimum(column + HALF, readout - 1) - jnp.maximum(column - HALF, 0) + 1
    weighted = acc_ref[...] * (covers_t * covers_x).astype(f32)
    trace = jnp.sum(jnp.sum(weighted, axis=1, keepdims=True), axis=0, keepdims=True)
    scale = trace / (SPAN**3 * coils) + 1e-06

    def product(left, right):
        both = lax.dot_general(left, right[: 2 * pad], NT, preferred_element_type=f32)
        cross = lax.dot_general(left[: 2 * band], right[2 * pad :], NT, preferred_element_type=f32)
        return both[: 2 * band] + both[2 * band :] + cross

    mrow = lax.broadcasted_iota(jnp.int32, (band, pad), 0) // coils % frames
    mcol = lax.broadcasted_iota(jnp.int32, (band, pad), 1) // coils % frames
    mixes = []
    for shift in range(-frames + 1, frames):
        mask = jnp.zeros((band, pad), f32)
        for i in range(frames):
            for j in range(frames):
                if 0 <= i + shift < frames and 0 <= j + shift < frames:
                    count = sum(
                        abs(i - t) <= HALF and abs(j - t) <= HALF and 0 <= t + shift < frames for t in range(frames)
                    )
                    mask = jnp.where((mrow == i) & (mcol == j), float(count), mask)
        mixes.append((shift, mask))

    def mixed(gram):
        total = None
        for shift, mask in mixes:
            moved = gram
            if shift:
                moved = pltpu.roll(pltpu.roll(gram, -shift * coils % pad, 1), -shift * coils % band, 0)
            total = moved * mask if total is None else total + moved * mask
        return total

    def complex_gram(stacked):
        real = stacked[:band, :pad] + stacked[band:, pad:]
        imag = stacked[:band, pad:] - stacked[band:, :pad]
        return mixed(real), mixed(imag)

    slot = 0
    order = []

    def put(real, imag, lag, weight):
        nonlocal slot
        lhs_ref[:band, slot * pad : (slot + 1) * pad] = real
        lhs_ref[band:, slot * pad : (slot + 1) * pad] = imag
        order.append((lag, weight))
        slot += 1

    def put_both(pair, lag, weight, back_weight):
        real, imag = pair
        put(real, imag, lag, weight)
        fill = jnp.zeros((pad - band, pad), f32)
        real_t = jnp.transpose(jnp.concatenate([real, fill], axis=0))[:band]
        imag_t = jnp.transpose(jnp.concatenate([imag, fill], axis=0))[:band]
        put(real_t, -imag_t, -lag, back_weight)

    window = lax.broadcasted_iota(jnp.int32, (cell, up(width, LANES)), 1)
    my_line = me * rows + window // readout
    valid = [((my_line - b + HALF >= 0) & (my_line - b + HALF < lines)).astype(f32) for b in range(SPAN)]

    def lag_weight(lag):
        total = None
        for b in range(SPAN):
            if 0 <= b + lag < SPAN:
                total = valid[b] if total is None else total + valid[b]
        return total

    depth = max(d for d in range(1, 17) if tiles % d == 0)
    for lag in range(SPAN):

        def part(step):
            left = z_ref[:, pl.ds(lane_tile(LAGS - lag + step * depth), depth * LANES)]
            right = zc_ref[:, pl.ds(lane_tile(step * depth), depth * LANES)]
            return product(left, right)

        if tiles == depth:
            stacked = part(0)
        else:
            stacked = lax.fori_loop(
                0, tiles // depth, lambda step, total: total + part(step), jnp.zeros((2 * band, 2 * pad), f32)
            )
        pair = complex_gram(stacked)
        if lag == 0:
            put(*pair, 0, lag_weight(0))
        else:
            put_both(pair, lag, lag_weight(lag), lag_weight(-lag))

    def edge(first, second):
        group, tile = divmod(first, tiles)
        other = second % tiles
        start = (LAGS + tile) * LANES
        here = lax.broadcasted_iota(jnp.int32, (4 * band, LANES), 1) // readout == group
        left = jnp.where(here, z_ref[:, start : start + LANES].astype(f32), 0.0).astype(jnp.bfloat16)
        return complex_gram(product(left, zc_ref[:, other * LANES : (other + 1) * LANES]))

    last = lines - 1
    put(*edge(last - 1, last - 1), 0, -valid[0])
    put(*edge(last, last), 0, -(valid[0] + valid[1]))
    put(*edge(0, 0), 0, -(valid[3] + valid[4]))
    put(*edge(1, 1), 0, -valid[4])
    put_both(edge(last - 1, last), 1, -valid[0], -valid[1])
    put_both(edge(0, 1), 1, -valid[3], -valid[4])

    reach = up(LAGS, rows) // rows
    for j in range(-reach, reach + 1):
        block = me + j
        exists = (block >= 0) & (block < slabs)
        block = jnp.clip(block, 0, slabs - 1)
        for line in range(rows):
            start = (j + reach) * width + line * readout
            for plane in range(planes):
                held = jnp.where(exists, unpacked(block, plane, line), 0.0)
                xw_ref[plane * coils : (plane + 1) * coils, start : start + readout] = held
    extent = xw_ref.shape[1]
    spread = lax.broadcasted_iota(jnp.int32, (2 * cell, extent), 1) % readout
    around = xw_ref[...]
    wide = up(width, LANES)
    for e in range(SPAN):
        moved = around if e == HALF else pltpu.roll(around, (HALF - e) % extent, 1)
        near = spread + e - HALF
        moved = jnp.where((near >= 0) & (near < readout), moved, 0.0)
        for lag in range(-LAGS, LAGS + 1):
            start = (reach * rows + lag) * readout
            piece = moved[:, start : start + wide]
            for index, (at, weight) in enumerate(order):
                if at == lag:
                    first = index * pad + e * cell
                    for part in range(2):
                        high, low = split(piece[part * cell : (part + 1) * cell] * weight)
                        rhs_ref[first : first + cell, part * wide : (part + 1) * wide] = high
                        rhs_ref[first : first + cell, (2 + part) * wide : (3 + part) * wide] = low
    for index in range(len(order)):
        first = index * pad
        rhs_ref[first + band : first + pad, :] = jnp.zeros((pad - band, 4 * wide), jnp.bfloat16)

    high, low = split(lhs_ref[...])
    lead = rhs_ref[:, : 2 * wide]
    total = lax.dot_general(high, lead, NN, preferred_element_type=f32)
    total += lax.dot_general(low, lead, NN, preferred_element_type=f32)
    total += lax.dot_general(high, rhs_ref[:, 2 * wide :], NN, preferred_element_type=f32)
    real = total[:band, :wide] + total[band:, wide:]
    imag = total[:band, wide:] - total[band:, :wide]

    factor = 1.0 / (SPAN**3 * scale)
    column = window % readout
    for part, values in enumerate((real, imag)):
        folded = jnp.zeros((cell, wide), f32)
        for e in range(SPAN):
            moved = values[e * cell : (e + 1) * cell]
            if e != HALF:
                moved = pltpu.roll(moved, (e - HALF) % wide, 1)
            near = column - e + HALF
            folded += jnp.where((near >= 0) & (near < readout), moved, 0.0)
        folded = folded * factor
        for line in range(rows):
            for f in range(frames):
                kept = measured_ref[part, :, line, f, :]
                at = (slice(f * coils, (f + 1) * coils), slice(line * readout, (line + 1) * readout))
                out_ref[part, :, line, f, :] = jnp.where(hit_ref[at] > 0, kept, folded[at])


def pack(lines_ref, estimate_ref, packed_ref, hit_ref):
    _, coils, rows, frames, readout = estimate_ref.shape
    shape = hit_ref.shape
    line = lax.axis_index("slab") * rows + lax.broadcasted_iota(jnp.int32, shape, 1) // readout
    frame = lax.broadcasted_iota(jnp.int32, shape, 0) // coils
    hit = jnp.zeros(shape, jnp.int32)
    for f in range(frames):
        for sample in range(lines_ref.shape[1]):
            hit = jnp.where((line == lines_ref[f, sample]) & (frame == f), 1, hit)
    hit_ref[...] = hit
    groups = LANES // readout
    for part in range(2):
        for f in range(frames):
            for line in range(rows):
                down, right = divmod((part * frames + f) * rows + line, groups)
                at = (slice(down * coils, (down + 1) * coils), slice(right * readout, (right + 1) * readout))
                packed_ref[at] = estimate_ref[part, :, line, f, :]


def nearby(slabs):
    return 4 if slabs % 4 == 0 else 1


def exchanged(block, groups):
    copies = jnp.broadcast_to(block[None], (len(groups[0]),) + block.shape)
    return lax.all_to_all(copies, "slab", 0, 0, axis_index_groups=groups)


def gather(block):
    slabs = lax.axis_size("slab")
    near = nearby(slabs)
    column = exchanged(block, [[i + j * near for j in range(slabs // near)] for i in range(near)])
    whole = exchanged(column, [[i * near + j for j in range(near)] for i in range(slabs // near)])
    return whole.reshape((slabs,) + block.shape)


def local(estimate, measured, sampled_lines):
    _, coils, frames, rows, readout = estimate.shape
    slabs = lax.axis_size("slab")
    cell = coils * frames
    width = rows * readout
    band = SPAN * cell
    pad = up(band, LANES)
    wide = up(width, LANES)
    groups = LANES // readout
    tiles = up(slabs * rows, groups) // groups
    reach = up(LAGS, rows) // rows
    slots = 2 * SPAN - 1 + 8

    vmem = pl.BlockSpec(memory_space=pltpu.VMEM)
    packed, hit = pl.pallas_call(
        pack,
        out_shape=(
            jax.ShapeDtypeStruct((up(2 * frames * rows, groups) // groups * coils, LANES), jnp.float32),
            jax.ShapeDtypeStruct((cell, wide), jnp.int32),
        ),
        in_specs=[pl.BlockSpec(memory_space=pltpu.SMEM), vmem],
        out_specs=(vmem, vmem),
        name="pack",
    )(sampled_lines, jnp.swapaxes(estimate, 2, 3))
    gathered = gather(packed)
    sizes = (slabs, coils, frames, rows, readout)
    result = pl.pallas_call(
        functools.partial(kernel, sizes),
        out_shape=jax.ShapeDtypeStruct((2, coils, rows, frames, readout), jnp.float32),
        in_specs=[vmem, vmem, vmem],
        out_specs=vmem,
        scratch_shapes=[
            pltpu.VMEM((2 * cell, (LAGS + tiles) * LANES), jnp.float32),
            pltpu.VMEM((4 * band, (LAGS + tiles) * LANES), jnp.bfloat16),
            pltpu.VMEM((4 * pad, tiles * LANES), jnp.bfloat16),
            pltpu.VMEM((2 * cell, LANES), jnp.float32),
            pltpu.VMEM((2 * cell, up((2 * reach + 1) * width + LANES, LANES)), jnp.float32),
            pltpu.VMEM((2 * band, slots * pad), jnp.float32),
            pltpu.VMEM((slots * pad, 4 * wide), jnp.bfloat16),
        ],
        compiler_params=pltpu.CompilerParams(vmem_limit_bytes=48 * 1024 * 1024),
        name="filter_step",
    )(hit, gathered, jnp.swapaxes(measured, 2, 3))
    return jnp.swapaxes(result, 2, 3)


def solution(mesh):
    placed = (
        P(None, None, "grp", "slab", None),
        P(None, None, "grp", "slab", None),
        P("grp", None),
    )
    return jax.shard_map(
        local,
        mesh=mesh,
        in_specs=placed,
        out_specs=P(None, None, "grp", "slab", None),
        check_vma=False,
    )
```

```python
import functools

import jax
import jax.numpy as jnp
from jax import lax
from jax.experimental import pallas as pl
from jax.experimental.pallas import tpu as pltpu
from jax.sharding import PartitionSpec as P

SPAN = 5
HALF = SPAN // 2
LAGS = SPAN - 1
LANES = 128
NT = (((1,), (1,)), ((), ()))
NN = (((1,), (0,)), ((), ()))


def up(size, unit):
    return -(-size // unit) * unit


def split(value):
    high = value.astype(jnp.bfloat16)
    return high, (value - high.astype(jnp.float32)).astype(jnp.bfloat16)


def repeat(count, body):
    if count <= 16:
        for step in range(count):
            body(step)
    else:
        lax.fori_loop(0, count, lambda step, carry: (body(step), carry)[1], 0)


def lane_tile(tile):
    start = tile * LANES
    return start if isinstance(start, int) else pl.multiple_of(start, LANES)


def kernel(sizes, hit_ref, gathered_ref, measured_ref, out_ref, x_ref, z_ref, zc_ref, acc_ref, xw_ref, lhs_ref, rhs_ref):
    slabs, coils, frames, rows, readout = sizes
    me = lax.axis_index("slab")
    cell = coils * frames
    band = SPAN * cell
    width = rows * readout
    groups = LANES // readout
    lines = slabs * rows
    tiles = up(lines, groups) // groups
    f32 = jnp.float32

    planes = 2 * frames

    def unpacked(block, plane, line):
        down, right = divmod(plane * rows + line, groups)
        return gathered_ref[block, down * coils : (down + 1) * coils, right * readout : (right + 1) * readout]

    if tiles * groups != lines:
        x_ref[...] = jnp.zeros_like(x_ref)
    for line in range(lines):
        block, inner = divmod(line, rows)
        group, tile = divmod(line, tiles)
        start = (LAGS + tile) * LANES + group * readout
        for plane in range(planes):
            x_ref[plane * coils : (plane + 1) * coils, start : start + readout] = unpacked(block, plane, inner)
    lane = lax.broadcasted_iota(jnp.int32, (2 * cell, LANES), 1)
    for back in range(1, LAGS + 1):
        source = (LAGS + tiles - back) * LANES
        wrapped = pltpu.roll(x_ref[:, source : source + LANES], readout, 1)
        target = (LAGS - back) * LANES
        x_ref[:, target : target + LANES] = jnp.where(lane >= readout, wrapped, 0.0)

    column = lane % readout
    inside = [(column + e - HALF >= 0) & (column + e - HALF < readout) for e in range(SPAN)]

    def patches(tile):
        at = pl.ds(lane_tile(tile), LANES)
        cells = x_ref[:, at]
        for e in range(SPAN):
            moved = cells if e == HALF else pltpu.roll(cells, (HALF - e) % LANES, 1)
            high, low = split(jnp.where(inside[e], moved, 0.0))
            for part in range(2):
                first = part * band + e * cell
                z_ref[first : first + cell, at] = high[part * cell : (part + 1) * cell]
                z_ref[2 * band + first : 2 * band + first + cell, at] = low[part * cell : (part + 1) * cell]

    repeat(LAGS + tiles, patches)

    pad = up(band, LANES)

    def centre(tile):
        source = pl.ds(lane_tile(tile + LAGS), LANES)
        at = pl.ds(lane_tile(tile), LANES)
        for piece in range(4):
            first = piece * pad
            zc_ref[first : first + band, at] = z_ref[piece * band : (piece + 1) * band, source]
            zc_ref[first + band : first + pad, at] = jnp.zeros((pad - band, LANES), jnp.bfloat16)

    repeat(tiles, centre)

    line_base = lane // readout * tiles
    acc_ref[...] = jnp.zeros_like(acc_ref)

    def energy(tile):
        cells = x_ref[:, pl.ds(lane_tile(tile + LAGS), LANES)]
        line = line_base + tile
        covers = jnp.minimum(line + HALF, lines - 1) - jnp.maximum(line - HALF, 0) + 1
        acc_ref[...] += cells * cells * covers.astype(f32)

    repeat(tiles, energy)
    row = lax.broadcasted_iota(jnp.int32, (2 * cell, LANES), 0)
    frame = row // coils % frames
    covers_t = jnp.minimum(frame + HALF, frames - 1) - jnp.maximum(frame - HALF, 0) + 1
    covers_x = jnp.minimum(column + HALF, readout - 1) - jnp.maximum(column - HALF, 0) + 1
    weighted = acc_ref[...] * (covers_t * covers_x).astype(f32)
    trace = jnp.sum(jnp.sum(weighted, axis=1, keepdims=True), axis=0, keepdims=True)
    scale = trace / (SPAN**3 * coils) + 1e-06

    def product(left, right):
        both = lax.dot_general(left, right[: 2 * pad], NT, preferred_element_type=f32)
        cross = lax.dot_general(left[: 2 * band], right[2 * pad :], NT, preferred_element_type=f32)
        return both[: 2 * band] + both[2 * band :] + cross

    mrow = lax.broadcasted_iota(jnp.int32, (band, pad), 0) // coils % frames
    mcol = lax.broadcasted_iota(jnp.int32, (band, pad), 1) // coils % frames
    mixes = []
    for shift in range(-frames + 1, frames):
        mask = jnp.zeros((band, pad), f32)
        for i in range(frames):
            for j in range(frames):
                if 0 <= i + shift < frames and 0 <= j + shift < frames:
                    count = sum(
                        abs(i - t) <= HALF and abs(j - t) <= HALF and 0 <= t + shift < frames for t in range(frames)
                    )
                    mask = jnp.where((mrow == i) & (mcol == j), float(count), mask)
        mixes.append((shift, mask))

    def mixed(gram):
        total = None
        for shift, mask in mixes:
            moved = gram
            if shift:
                moved = pltpu.roll(pltpu.roll(gram, -shift * coils % pad, 1), -shift * coils % band, 0)
            total = moved * mask if total is None else total + moved * mask
        return total

    def complex_gram(stacked):
        real = stacked[:band, :pad] + stacked[band:, pad:]
        imag = stacked[:band, pad:] - stacked[band:, :pad]
        return mixed(real), mixed(imag)

    slot = 0
    order = []

    def put(real, imag, lag, weight):
        nonlocal slot
        lhs_ref[:band, slot * pad : (slot + 1) * pad] = real
        lhs_ref[band:, slot * pad : (slot + 1) * pad] = imag
        order.append((lag, weight))
        slot += 1

    def put_both(pair, lag, weight, back_weight):
        real, imag = pair
        put(real, imag, lag, weight)
        fill = jnp.zeros((pad - band, pad), f32)
        real_t = jnp.transpose(jnp.concatenate([real, fill], axis=0))[:band]
        imag_t = jnp.transpose(jnp.concatenate([imag, fill], axis=0))[:band]
        put(real_t, -imag_t, -lag, back_weight)

    window = lax.broadcasted_iota(jnp.int32, (cell, up(width, LANES)), 1)
    my_line = me * rows + window // readout
    valid = [((my_line - b + HALF >= 0) & (my_line - b + HALF < lines)).astype(f32) for b in range(SPAN)]

    def lag_weight(lag):
        total = None
        for b in range(SPAN):
            if 0 <= b + lag < SPAN:
                total = valid[b] if total is None else total + valid[b]
        return total

    depth = max(d for d in range(1, 17) if tiles % d == 0)
    for lag in range(SPAN):

        def part(step):
            left = z_ref[:, pl.ds(lane_tile(LAGS - lag + step * depth), depth * LANES)]
            right = zc_ref[:, pl.ds(lane_tile(step * depth), depth * LANES)]
            return product(left, right)

        if tiles == depth:
            stacked = part(0)
        else:
            stacked = lax.fori_loop(
                0, tiles // depth, lambda step, total: total + part(step), jnp.zeros((2 * band, 2 * pad), f32)
            )
        pair = complex_gram(stacked)
        if lag == 0:
            put(*pair, 0, lag_weight(0))
        else:
            put_both(pair, lag, lag_weight(lag), lag_weight(-lag))

    def edge(first, second):
        group, tile = divmod(first, tiles)
        other = second % tiles
        start = (LAGS + tile) * LANES
        here = lax.broadcasted_iota(jnp.int32, (4 * band, LANES), 1) // readout == group
        left = jnp.where(here, z_ref[:, start : start + LANES].astype(f32), 0.0).astype(jnp.bfloat16)
        return complex_gram(product(left, zc_ref[:, other * LANES : (other + 1) * LANES]))

    last = lines - 1
    put(*edge(last - 1, last - 1), 0, -valid[0])
    put(*edge(last, last), 0, -(valid[0] + valid[1]))
    put(*edge(0, 0), 0, -(valid[3] + valid[4]))
    put(*edge(1, 1), 0, -valid[4])
    put_both(edge(last - 1, last), 1, -valid[0], -valid[1])
    put_both(edge(0, 1), 1, -valid[3], -valid[4])

    reach = up(LAGS, rows) // rows
    for j in range(-reach, reach + 1):
        block = me + j
        exists = (block >= 0) & (block < slabs)
        block = jnp.clip(block, 0, slabs - 1)
        for line in range(rows):
            start = (j + reach) * width + line * readout
            for plane in range(planes):
                held = jnp.where(exists, unpacked(block, plane, line), 0.0)
                xw_ref[plane * coils : (plane + 1) * coils, start : start + readout] = held
    extent = xw_ref.shape[1]
    spread = lax.broadcasted_iota(jnp.int32, (2 * cell, extent), 1) % readout
    around = xw_ref[...]
    wide = up(width, LANES)
    for e in range(SPAN):
        moved = around if e == HALF else pltpu.roll(around, (HALF - e) % extent, 1)
        near = spread + e - HALF
        moved = jnp.where((near >= 0) & (near < readout), moved, 0.0)
        for lag in range(-LAGS, LAGS + 1):
            start = (reach * rows + lag) * readout
            piece = moved[:, start : start + wide]
            for index, (at, weight) in enumerate(order):
                if at == lag:
                    first = index * pad + e * cell
                    for part in range(2):
                        high, low = split(piece[part * cell : (part + 1) * cell] * weight)
                        rhs_ref[first : first + cell, part * wide : (part + 1) * wide] = high
                        rhs_ref[first : first + cell, (2 + part) * wide : (3 + part) * wide] = low
    for index in range(len(order)):
        first = index * pad
        rhs_ref[first + band : first + pad, :] = jnp.zeros((pad - band, 4 * wide), jnp.bfloat16)

    high, low = split(lhs_ref[...])
    lead = rhs_ref[:, : 2 * wide]
    total = lax.dot_general(high, lead, NN, preferred_element_type=f32)
    total += lax.dot_general(low, lead, NN, preferred_element_type=f32)
    total += lax.dot_general(high, rhs_ref[:, 2 * wide :], NN, preferred_element_type=f32)
    real = total[:band, :wide] + total[band:, wide:]
    imag = total[:band, wide:] - total[band:, :wide]

    factor = 1.0 / (SPAN**3 * scale)
    column = window % readout
    for part, values in enumerate((real, imag)):
        folded = jnp.zeros((cell, wide), f32)
        for e in range(SPAN):
            moved = values[e * cell : (e + 1) * cell]
            if e != HALF:
                moved = pltpu.roll(moved, (e - HALF) % wide, 1)
            near = column - e + HALF
            folded += jnp.where((near >= 0) & (near < readout), moved, 0.0)
        folded = folded * factor
        for line in range(rows):
            for f in range(frames):
                kept = measured_ref[part, :, line, f, :]
                at = (slice(f * coils, (f + 1) * coils), slice(line * readout, (line + 1) * readout))
                out_ref[part, :, line, f, :] = jnp.where(hit_ref[at] > 0, kept, folded[at])


def pack(lines_ref, estimate_ref, packed_ref, hit_ref):
    _, coils, rows, frames, readout = estimate_ref.shape
    shape = hit_ref.shape
    line = lax.axis_index("slab") * rows + lax.broadcasted_iota(jnp.int32, shape, 1) // readout
    frame = lax.broadcasted_iota(jnp.int32, shape, 0) // coils
    hit = jnp.zeros(shape, jnp.int32)
    for f in range(frames):
        for sample in range(lines_ref.shape[1]):
            hit = jnp.where((line == lines_ref[f, sample]) & (frame == f), 1, hit)
    hit_ref[...] = hit
    groups = LANES // readout
    for part in range(2):
        for f in range(frames):
            for line in range(rows):
                down, right = divmod((part * frames + f) * rows + line, groups)
                at = (slice(down * coils, (down + 1) * coils), slice(right * readout, (right + 1) * readout))
                packed_ref[at] = estimate_ref[part, :, line, f, :]


def gather(block):
    copies = jnp.broadcast_to(block[None], (lax.axis_size("slab"),) + block.shape)
    return lax.all_to_all(copies, "slab", 0, 0)


def local(estimate, measured, sampled_lines):
    _, coils, frames, rows, readout = estimate.shape
    slabs = lax.axis_size("slab")
    cell = coils * frames
    width = rows * readout
    band = SPAN * cell
    pad = up(band, LANES)
    wide = up(width, LANES)
    groups = LANES // readout
    tiles = up(slabs * rows, groups) // groups
    reach = up(LAGS, rows) // rows
    slots = 2 * SPAN - 1 + 8

    vmem = pl.BlockSpec(memory_space=pltpu.VMEM)
    packed, hit = pl.pallas_call(
        pack,
        out_shape=(
            jax.ShapeDtypeStruct((up(2 * frames * rows, groups) // groups * coils, LANES), jnp.float32),
            jax.ShapeDtypeStruct((cell, wide), jnp.int32),
        ),
        in_specs=[pl.BlockSpec(memory_space=pltpu.SMEM), vmem],
        out_specs=(vmem, vmem),
        compiler_params=pltpu.CompilerParams(vmem_limit_bytes=2 * 1024 * 1024),
        name="pack",
    )(sampled_lines, jnp.swapaxes(estimate, 2, 3))
    gathered = gather(packed)
    sizes = (slabs, coils, frames, rows, readout)
    result = pl.pallas_call(
        functools.partial(kernel, sizes),
        out_shape=jax.ShapeDtypeStruct((2, coils, rows, frames, readout), jnp.float32),
        in_specs=[vmem, vmem, vmem],
        out_specs=vmem,
        scratch_shapes=[
            pltpu.VMEM((2 * cell, (LAGS + tiles) * LANES), jnp.float32),
            pltpu.VMEM((4 * band, (LAGS + tiles) * LANES), jnp.bfloat16),
            pltpu.VMEM((4 * pad, tiles * LANES), jnp.bfloat16),
            pltpu.VMEM((2 * cell, LANES), jnp.float32),
            pltpu.VMEM((2 * cell, up((2 * reach + 1) * width + LANES, LANES)), jnp.float32),
            pltpu.VMEM((2 * band, slots * pad), jnp.float32),
            pltpu.VMEM((slots * pad, 4 * wide), jnp.bfloat16),
        ],
        compiler_params=pltpu.CompilerParams(vmem_limit_bytes=40 * 1024 * 1024),
        name="filter_step",
    )(hit, gathered, jnp.swapaxes(measured, 2, 3))
    return jnp.swapaxes(result, 2, 3)


def solution(mesh):
    placed = (
        P(None, None, "grp", "slab", None),
        P(None, None, "grp", "slab", None),
        P("grp", None),
    )
    return jax.shard_map(
        local,
        mesh=mesh,
        in_specs=placed,
        out_specs=P(None, None, "grp", "slab", None),
        check_vma=False,
    )
```

```python
import functools

import jax
import jax.numpy as jnp
from jax import lax
from jax.experimental import pallas as pl
from jax.experimental.pallas import tpu as pltpu
from jax.sharding import PartitionSpec as P

SPAN = 5
HALF = SPAN // 2
LAGS = SPAN - 1
LANES = 128
NT = (((1,), (1,)), ((), ()))
NN = (((1,), (0,)), ((), ()))


def up(size, unit):
    return -(-size // unit) * unit


def split(value):
    high = value.astype(jnp.bfloat16)
    return high, (value - high.astype(jnp.float32)).astype(jnp.bfloat16)


def repeat(count, body):
    if count <= 16:
        for step in range(count):
            body(step)
    else:
        lax.fori_loop(0, count, lambda step, carry: (body(step), carry)[1], 0)


def lane_tile(tile):
    start = tile * LANES
    return start if isinstance(start, int) else pl.multiple_of(start, LANES)


def kernel(sizes, hit_ref, gathered_ref, measured_ref, out_ref, x_ref, z_ref, zc_ref, acc_ref, xw_ref, lhs_ref, rhs_ref):
    slabs, coils, frames, rows, readout = sizes
    me = lax.axis_index("slab")
    cell = coils * frames
    band = SPAN * cell
    width = rows * readout
    groups = LANES // readout
    lines = slabs * rows
    tiles = up(lines, groups) // groups
    f32 = jnp.float32

    planes = 2 * frames

    def unpacked(block, plane, line):
        down, right = divmod(plane * rows + line, groups)
        return gathered_ref[block, down * coils : (down + 1) * coils, right * readout : (right + 1) * readout]

    if tiles * groups != lines:
        x_ref[...] = jnp.zeros_like(x_ref)
    for line in range(lines):
        block, inner = divmod(line, rows)
        group, tile = divmod(line, tiles)
        start = (LAGS + tile) * LANES + group * readout
        for plane in range(planes):
            x_ref[plane * coils : (plane + 1) * coils, start : start + readout] = unpacked(block, plane, inner)
    lane = lax.broadcasted_iota(jnp.int32, (2 * cell, LANES), 1)
    for back in range(1, LAGS + 1):
        source = (LAGS + tiles - back) * LANES
        wrapped = pltpu.roll(x_ref[:, source : source + LANES], readout, 1)
        target = (LAGS - back) * LANES
        x_ref[:, target : target + LANES] = jnp.where(lane >= readout, wrapped, 0.0)

    column = lane % readout
    inside = [(column + e - HALF >= 0) & (column + e - HALF < readout) for e in range(SPAN)]

    def patches(tile):
        at = pl.ds(lane_tile(tile), LANES)
        cells = x_ref[:, at]
        for e in range(SPAN):
            moved = cells if e == HALF else pltpu.roll(cells, (HALF - e) % LANES, 1)
            high, low = split(jnp.where(inside[e], moved, 0.0))
            for part in range(2):
                first = part * band + e * cell
                z_ref[first : first + cell, at] = high[part * cell : (part + 1) * cell]
                z_ref[2 * band + first : 2 * band + first + cell, at] = low[part * cell : (part + 1) * cell]

    repeat(LAGS + tiles, patches)

    pad = up(band, LANES)

    def centre(tile):
        source = pl.ds(lane_tile(tile + LAGS), LANES)
        at = pl.ds(lane_tile(tile), LANES)
        for piece in range(4):
            first = piece * pad
            zc_ref[first : first + band, at] = z_ref[piece * band : (piece + 1) * band, source]
            zc_ref[first + band : first + pad, at] = jnp.zeros((pad - band, LANES), jnp.bfloat16)

    repeat(tiles, centre)

    line_base = lane // readout * tiles
    acc_ref[...] = jnp.zeros_like(acc_ref)

    def energy(tile):
        cells = x_ref[:, pl.ds(lane_tile(tile + LAGS), LANES)]
        line = line_base + tile
        covers = jnp.minimum(line + HALF, lines - 1) - jnp.maximum(line - HALF, 0) + 1
        acc_ref[...] += cells * cells * covers.astype(f32)

    repeat(tiles, energy)
    row = lax.broadcasted_iota(jnp.int32, (2 * cell, LANES), 0)
    frame = row // coils % frames
    covers_t = jnp.minimum(frame + HALF, frames - 1) - jnp.maximum(frame - HALF, 0) + 1
    covers_x = jnp.minimum(column + HALF, readout - 1) - jnp.maximum(column - HALF, 0) + 1
    weighted = acc_ref[...] * (covers_t * covers_x).astype(f32)
    trace = jnp.sum(jnp.sum(weighted, axis=1, keepdims=True), axis=0, keepdims=True)
    scale = trace / (SPAN**3 * coils) + 1e-06

    def product(left, right):
        both = lax.dot_general(left, right[: 2 * pad], NT, preferred_element_type=f32)
        cross = lax.dot_general(left[: 2 * band], right[2 * pad :], NT, preferred_element_type=f32)
        return both[: 2 * band] + both[2 * band :] + cross

    mrow = lax.broadcasted_iota(jnp.int32, (band, pad), 0) // coils % frames
    mcol = lax.broadcasted_iota(jnp.int32, (band, pad), 1) // coils % frames
    mixes = []
    for shift in range(-frames + 1, frames):
        mask = jnp.zeros((band, pad), f32)
        for i in range(frames):
            for j in range(frames):
                if 0 <= i + shift < frames and 0 <= j + shift < frames:
                    count = sum(
                        abs(i - t) <= HALF and abs(j - t) <= HALF and 0 <= t + shift < frames for t in range(frames)
                    )
                    mask = jnp.where((mrow == i) & (mcol == j), float(count), mask)
        mixes.append((shift, mask))

    def mixed(gram):
        total = None
        for shift, mask in mixes:
            moved = gram
            if shift:
                moved = pltpu.roll(pltpu.roll(gram, -shift * coils % pad, 1), -shift * coils % band, 0)
            total = moved * mask if total is None else total + moved * mask
        return total

    def complex_gram(stacked):
        real = stacked[:band, :pad] + stacked[band:, pad:]
        imag = stacked[:band, pad:] - stacked[band:, :pad]
        return mixed(real), mixed(imag)

    slot = 0
    order = []

    def put(real, imag, lag, weight):
        nonlocal slot
        lhs_ref[:band, slot * pad : (slot + 1) * pad] = real
        lhs_ref[band:, slot * pad : (slot + 1) * pad] = imag
        order.append((lag, weight))
        slot += 1

    def put_both(pair, lag, weight, back_weight):
        real, imag = pair
        put(real, imag, lag, weight)
        fill = jnp.zeros((pad - band, pad), f32)
        real_t = jnp.transpose(jnp.concatenate([real, fill], axis=0))[:band]
        imag_t = jnp.transpose(jnp.concatenate([imag, fill], axis=0))[:band]
        put(real_t, -imag_t, -lag, back_weight)

    window = lax.broadcasted_iota(jnp.int32, (cell, up(width, LANES)), 1)
    my_line = me * rows + window // readout
    valid = [((my_line - b + HALF >= 0) & (my_line - b + HALF < lines)).astype(f32) for b in range(SPAN)]

    def lag_weight(lag):
        total = None
        for b in range(SPAN):
            if 0 <= b + lag < SPAN:
                total = valid[b] if total is None else total + valid[b]
        return total

    depth = max(d for d in range(1, 17) if tiles % d == 0)
    for lag in range(SPAN):

        def part(step):
            left = z_ref[:, pl.ds(lane_tile(LAGS - lag + step * depth), depth * LANES)]
            right = zc_ref[:, pl.ds(lane_tile(step * depth), depth * LANES)]
            return product(left, right)

        if tiles == depth:
            stacked = part(0)
        else:
            stacked = lax.fori_loop(
                0, tiles // depth, lambda step, total: total + part(step), jnp.zeros((2 * band, 2 * pad), f32)
            )
        pair = complex_gram(stacked)
        if lag == 0:
            put(*pair, 0, lag_weight(0))
        else:
            put_both(pair, lag, lag_weight(lag), lag_weight(-lag))

    def edge(first, second):
        group, tile = divmod(first, tiles)
        other = second % tiles
        start = (LAGS + tile) * LANES
        here = lax.broadcasted_iota(jnp.int32, (4 * band, LANES), 1) // readout == group
        left = jnp.where(here, z_ref[:, start : start + LANES].astype(f32), 0.0).astype(jnp.bfloat16)
        return complex_gram(product(left, zc_ref[:, other * LANES : (other + 1) * LANES]))

    last = lines - 1
    put(*edge(last - 1, last - 1), 0, -valid[0])
    put(*edge(last, last), 0, -(valid[0] + valid[1]))
    put(*edge(0, 0), 0, -(valid[3] + valid[4]))
    put(*edge(1, 1), 0, -valid[4])
    put_both(edge(last - 1, last), 1, -valid[0], -valid[1])
    put_both(edge(0, 1), 1, -valid[3], -valid[4])

    reach = up(LAGS, rows) // rows
    for j in range(-reach, reach + 1):
        block = me + j
        exists = (block >= 0) & (block < slabs)
        block = jnp.clip(block, 0, slabs - 1)
        for line in range(rows):
            start = (j + reach) * width + line * readout
            for plane in range(planes):
                held = jnp.where(exists, unpacked(block, plane, line), 0.0)
                xw_ref[plane * coils : (plane + 1) * coils, start : start + readout] = held
    extent = xw_ref.shape[1]
    spread = lax.broadcasted_iota(jnp.int32, (2 * cell, extent), 1) % readout
    around = xw_ref[...]
    wide = up(width, LANES)
    for e in range(SPAN):
        moved = around if e == HALF else pltpu.roll(around, (HALF - e) % extent, 1)
        near = spread + e - HALF
        moved = jnp.where((near >= 0) & (near < readout), moved, 0.0)
        for lag in range(-LAGS, LAGS + 1):
            start = (reach * rows + lag) * readout
            piece = moved[:, start : start + wide]
            for index, (at, weight) in enumerate(order):
                if at == lag:
                    first = index * pad + e * cell
                    for part in range(2):
                        high, low = split(piece[part * cell : (part + 1) * cell] * weight)
                        rhs_ref[first : first + cell, part * wide : (part + 1) * wide] = high
                        rhs_ref[first : first + cell, (2 + part) * wide : (3 + part) * wide] = low
    for index in range(len(order)):
        first = index * pad
        rhs_ref[first + band : first + pad, :] = jnp.zeros((pad - band, 4 * wide), jnp.bfloat16)

    high, low = split(lhs_ref[...])
    lead = rhs_ref[:, : 2 * wide]
    total = lax.dot_general(high, lead, NN, preferred_element_type=f32)
    total += lax.dot_general(low, lead, NN, preferred_element_type=f32)
    total += lax.dot_general(high, rhs_ref[:, 2 * wide :], NN, preferred_element_type=f32)
    real = total[:band, :wide] + total[band:, wide:]
    imag = total[:band, wide:] - total[band:, :wide]

    factor = 1.0 / (SPAN**3 * scale)
    column = window % readout
    for part, values in enumerate((real, imag)):
        folded = jnp.zeros((cell, wide), f32)
        for e in range(SPAN):
            moved = values[e * cell : (e + 1) * cell]
            if e != HALF:
                moved = pltpu.roll(moved, (e - HALF) % wide, 1)
            near = column - e + HALF
            folded += jnp.where((near >= 0) & (near < readout), moved, 0.0)
        folded = folded * factor
        for line in range(rows):
            for f in range(frames):
                kept = measured_ref[part, :, line, f, :]
                at = (slice(f * coils, (f + 1) * coils), slice(line * readout, (line + 1) * readout))
                out_ref[part, :, line, f, :] = jnp.where(hit_ref[at] > 0, kept, folded[at])


def pack(lines_ref, estimate_ref, packed_ref, hit_ref):
    _, coils, rows, frames, readout = estimate_ref.shape
    shape = hit_ref.shape
    line = lax.axis_index("slab") * rows + lax.broadcasted_iota(jnp.int32, shape, 1) // readout
    frame = lax.broadcasted_iota(jnp.int32, shape, 0) // coils
    hit = jnp.zeros(shape, jnp.int32)
    for f in range(frames):
        for sample in range(lines_ref.shape[1]):
            hit = jnp.where((line == lines_ref[f, sample]) & (frame == f), 1, hit)
    hit_ref[...] = hit
    groups = LANES // readout
    for part in range(2):
        for f in range(frames):
            for line in range(rows):
                down, right = divmod((part * frames + f) * rows + line, groups)
                at = (slice(down * coils, (down + 1) * coils), slice(right * readout, (right + 1) * readout))
                packed_ref[at] = estimate_ref[part, :, line, f, :]


def gather(block):
    return lax.all_gather(block, "slab")


def local(estimate, measured, sampled_lines):
    _, coils, frames, rows, readout = estimate.shape
    slabs = lax.axis_size("slab")
    cell = coils * frames
    width = rows * readout
    band = SPAN * cell
    pad = up(band, LANES)
    wide = up(width, LANES)
    groups = LANES // readout
    tiles = up(slabs * rows, groups) // groups
    reach = up(LAGS, rows) // rows
    slots = 2 * SPAN - 1 + 8

    vmem = pl.BlockSpec(memory_space=pltpu.VMEM)
    packed, hit = pl.pallas_call(
        pack,
        out_shape=(
            jax.ShapeDtypeStruct((up(2 * frames * rows, groups) // groups * coils, LANES), jnp.float32),
            jax.ShapeDtypeStruct((cell, wide), jnp.int32),
        ),
        in_specs=[pl.BlockSpec(memory_space=pltpu.SMEM), vmem],
        out_specs=(vmem, vmem),
        compiler_params=pltpu.CompilerParams(vmem_limit_bytes=56 * 1024 * 1024),
        name="pack",
    )(sampled_lines, jnp.swapaxes(estimate, 2, 3))
    gathered = gather(packed)
    sizes = (slabs, coils, frames, rows, readout)
    result = pl.pallas_call(
        functools.partial(kernel, sizes),
        out_shape=jax.ShapeDtypeStruct((2, coils, rows, frames, readout), jnp.float32),
        in_specs=[vmem, vmem, vmem],
        out_specs=vmem,
        scratch_shapes=[
            pltpu.VMEM((2 * cell, (LAGS + tiles) * LANES), jnp.float32),
            pltpu.VMEM((4 * band, (LAGS + tiles) * LANES), jnp.bfloat16),
            pltpu.VMEM((4 * pad, tiles * LANES), jnp.bfloat16),
            pltpu.VMEM((2 * cell, LANES), jnp.float32),
            pltpu.VMEM((2 * cell, up((2 * reach + 1) * width + LANES, LANES)), jnp.float32),
            pltpu.VMEM((2 * band, slots * pad), jnp.float32),
            pltpu.VMEM((slots * pad, 4 * wide), jnp.bfloat16),
        ],
        compiler_params=pltpu.CompilerParams(vmem_limit_bytes=40 * 1024 * 1024),
        name="filter_step",
    )(hit, gathered, jnp.swapaxes(measured, 2, 3))
    return jnp.swapaxes(result, 2, 3)


def solution(mesh):
    placed = (
        P(None, None, "grp", "slab", None),
        P(None, None, "grp", "slab", None),
        P("grp", None),
    )
    return jax.shard_map(
        local,
        mesh=mesh,
        in_specs=placed,
        out_specs=P(None, None, "grp", "slab", None),
        check_vma=False,
    )
```

```python
import functools

import jax
import jax.numpy as jnp
from jax import lax
from jax.experimental import pallas as pl
from jax.experimental.pallas import tpu as pltpu
from jax.sharding import PartitionSpec as P

SPAN = 5
HALF = SPAN // 2
LAGS = SPAN - 1
LANES = 128
NT = (((1,), (1,)), ((), ()))
NN = (((1,), (0,)), ((), ()))


def up(size, unit):
    return -(-size // unit) * unit


def split(value):
    high = value.astype(jnp.bfloat16)
    return high, (value - high.astype(jnp.float32)).astype(jnp.bfloat16)


def repeat(count, body):
    if count <= 16:
        for step in range(count):
            body(step)
    else:
        lax.fori_loop(0, count, lambda step, carry: (body(step), carry)[1], 0)


def lane_tile(tile):
    start = tile * LANES
    return start if isinstance(start, int) else pl.multiple_of(start, LANES)


def kernel(sizes, hit_ref, gathered_ref, measured_ref, out_ref, x_ref, z_ref, zc_ref, acc_ref, xw_ref, lhs_ref, rhs_ref):
    slabs, coils, frames, rows, readout = sizes
    me = lax.axis_index("slab")
    cell = coils * frames
    band = SPAN * cell
    width = rows * readout
    groups = LANES // readout
    lines = slabs * rows
    tiles = up(lines, groups) // groups
    f32 = jnp.float32

    planes = 2 * frames

    def unpacked(block, plane, line):
        down, right = divmod(plane * rows + line, groups)
        return gathered_ref[place(block, slabs), down * coils : (down + 1) * coils, right * readout : (right + 1) * readout]

    if tiles * groups != lines:
        x_ref[...] = jnp.zeros_like(x_ref)
    for line in range(lines):
        block, inner = divmod(line, rows)
        group, tile = divmod(line, tiles)
        start = (LAGS + tile) * LANES + group * readout
        for plane in range(planes):
            x_ref[plane * coils : (plane + 1) * coils, start : start + readout] = unpacked(block, plane, inner)
    lane = lax.broadcasted_iota(jnp.int32, (2 * cell, LANES), 1)
    for back in range(1, LAGS + 1):
        source = (LAGS + tiles - back) * LANES
        wrapped = pltpu.roll(x_ref[:, source : source + LANES], readout, 1)
        target = (LAGS - back) * LANES
        x_ref[:, target : target + LANES] = jnp.where(lane >= readout, wrapped, 0.0)

    column = lane % readout
    inside = [(column + e - HALF >= 0) & (column + e - HALF < readout) for e in range(SPAN)]

    def patches(tile):
        at = pl.ds(lane_tile(tile), LANES)
        cells = x_ref[:, at]
        for e in range(SPAN):
            moved = cells if e == HALF else pltpu.roll(cells, (HALF - e) % LANES, 1)
            high, low = split(jnp.where(inside[e], moved, 0.0))
            for part in range(2):
                first = part * band + e * cell
                z_ref[first : first + cell, at] = high[part * cell : (part + 1) * cell]
                z_ref[2 * band + first : 2 * band + first + cell, at] = low[part * cell : (part + 1) * cell]

    repeat(LAGS + tiles, patches)

    pad = up(band, LANES)

    def centre(tile):
        source = pl.ds(lane_tile(tile + LAGS), LANES)
        at = pl.ds(lane_tile(tile), LANES)
        for piece in range(4):
            first = piece * pad
            zc_ref[first : first + band, at] = z_ref[piece * band : (piece + 1) * band, source]
            zc_ref[first + band : first + pad, at] = jnp.zeros((pad - band, LANES), jnp.bfloat16)

    repeat(tiles, centre)

    line_base = lane // readout * tiles
    acc_ref[...] = jnp.zeros_like(acc_ref)

    def energy(tile):
        cells = x_ref[:, pl.ds(lane_tile(tile + LAGS), LANES)]
        line = line_base + tile
        covers = jnp.minimum(line + HALF, lines - 1) - jnp.maximum(line - HALF, 0) + 1
        acc_ref[...] += cells * cells * covers.astype(f32)

    repeat(tiles, energy)
    row = lax.broadcasted_iota(jnp.int32, (2 * cell, LANES), 0)
    frame = row // coils % frames
    covers_t = jnp.minimum(frame + HALF, frames - 1) - jnp.maximum(frame - HALF, 0) + 1
    covers_x = jnp.minimum(column + HALF, readout - 1) - jnp.maximum(column - HALF, 0) + 1
    weighted = acc_ref[...] * (covers_t * covers_x).astype(f32)
    trace = jnp.sum(jnp.sum(weighted, axis=1, keepdims=True), axis=0, keepdims=True)
    scale = trace / (SPAN**3 * coils) + 1e-06

    def product(left, right):
        both = lax.dot_general(left, right[: 2 * pad], NT, preferred_element_type=f32)
        cross = lax.dot_general(left[: 2 * band], right[2 * pad :], NT, preferred_element_type=f32)
        return both[: 2 * band] + both[2 * band :] + cross

    mrow = lax.broadcasted_iota(jnp.int32, (band, pad), 0) // coils % frames
    mcol = lax.broadcasted_iota(jnp.int32, (band, pad), 1) // coils % frames
    mixes = []
    for shift in range(-frames + 1, frames):
        mask = jnp.zeros((band, pad), f32)
        for i in range(frames):
            for j in range(frames):
                if 0 <= i + shift < frames and 0 <= j + shift < frames:
                    count = sum(
                        abs(i - t) <= HALF and abs(j - t) <= HALF and 0 <= t + shift < frames for t in range(frames)
                    )
                    mask = jnp.where((mrow == i) & (mcol == j), float(count), mask)
        mixes.append((shift, mask))

    def mixed(gram):
        total = None
        for shift, mask in mixes:
            moved = gram
            if shift:
                moved = pltpu.roll(pltpu.roll(gram, -shift * coils % pad, 1), -shift * coils % band, 0)
            total = moved * mask if total is None else total + moved * mask
        return total

    def complex_gram(stacked):
        real = stacked[:band, :pad] + stacked[band:, pad:]
        imag = stacked[:band, pad:] - stacked[band:, :pad]
        return mixed(real), mixed(imag)

    slot = 0
    order = []

    def put(real, imag, lag, weight):
        nonlocal slot
        lhs_ref[:band, slot * pad : (slot + 1) * pad] = real
        lhs_ref[band:, slot * pad : (slot + 1) * pad] = imag
        order.append((lag, weight))
        slot += 1

    def put_both(pair, lag, weight, back_weight):
        real, imag = pair
        put(real, imag, lag, weight)
        fill = jnp.zeros((pad - band, pad), f32)
        real_t = jnp.transpose(jnp.concatenate([real, fill], axis=0))[:band]
        imag_t = jnp.transpose(jnp.concatenate([imag, fill], axis=0))[:band]
        put(real_t, -imag_t, -lag, back_weight)

    window = lax.broadcasted_iota(jnp.int32, (cell, up(width, LANES)), 1)
    my_line = me * rows + window // readout
    valid = [((my_line - b + HALF >= 0) & (my_line - b + HALF < lines)).astype(f32) for b in range(SPAN)]

    def lag_weight(lag):
        total = None
        for b in range(SPAN):
            if 0 <= b + lag < SPAN:
                total = valid[b] if total is None else total + valid[b]
        return total

    depth = max(d for d in range(1, 17) if tiles % d == 0)
    for lag in range(SPAN):

        def part(step):
            left = z_ref[:, pl.ds(lane_tile(LAGS - lag + step * depth), depth * LANES)]
            right = zc_ref[:, pl.ds(lane_tile(step * depth), depth * LANES)]
            return product(left, right)

        if tiles == depth:
            stacked = part(0)
        else:
            stacked = lax.fori_loop(
                0, tiles // depth, lambda step, total: total + part(step), jnp.zeros((2 * band, 2 * pad), f32)
            )
        pair = complex_gram(stacked)
        if lag == 0:
            put(*pair, 0, lag_weight(0))
        else:
            put_both(pair, lag, lag_weight(lag), lag_weight(-lag))

    def edge(first, second):
        group, tile = divmod(first, tiles)
        other = second % tiles
        start = (LAGS + tile) * LANES
        here = lax.broadcasted_iota(jnp.int32, (4 * band, LANES), 1) // readout == group
        left = jnp.where(here, z_ref[:, start : start + LANES].astype(f32), 0.0).astype(jnp.bfloat16)
        return complex_gram(product(left, zc_ref[:, other * LANES : (other + 1) * LANES]))

    last = lines - 1
    put(*edge(last - 1, last - 1), 0, -valid[0])
    put(*edge(last, last), 0, -(valid[0] + valid[1]))
    put(*edge(0, 0), 0, -(valid[3] + valid[4]))
    put(*edge(1, 1), 0, -valid[4])
    put_both(edge(last - 1, last), 1, -valid[0], -valid[1])
    put_both(edge(0, 1), 1, -valid[3], -valid[4])

    reach = up(LAGS, rows) // rows
    for j in range(-reach, reach + 1):
        block = me + j
        exists = (block >= 0) & (block < slabs)
        block = jnp.clip(block, 0, slabs - 1)
        for line in range(rows):
            start = (j + reach) * width + line * readout
            for plane in range(planes):
                held = jnp.where(exists, unpacked(block, plane, line), 0.0)
                xw_ref[plane * coils : (plane + 1) * coils, start : start + readout] = held
    extent = xw_ref.shape[1]
    spread = lax.broadcasted_iota(jnp.int32, (2 * cell, extent), 1) % readout
    around = xw_ref[...]
    wide = up(width, LANES)
    for e in range(SPAN):
        moved = around if e == HALF else pltpu.roll(around, (HALF - e) % extent, 1)
        near = spread + e - HALF
        moved = jnp.where((near >= 0) & (near < readout), moved, 0.0)
        for lag in range(-LAGS, LAGS + 1):
            start = (reach * rows + lag) * readout
            piece = moved[:, start : start + wide]
            for index, (at, weight) in enumerate(order):
                if at == lag:
                    first = index * pad + e * cell
                    for part in range(2):
                        high, low = split(piece[part * cell : (part + 1) * cell] * weight)
                        rhs_ref[first : first + cell, part * wide : (part + 1) * wide] = high
                        rhs_ref[first : first + cell, (2 + part) * wide : (3 + part) * wide] = low
    for index in range(len(order)):
        first = index * pad
        rhs_ref[first + band : first + pad, :] = jnp.zeros((pad - band, 4 * wide), jnp.bfloat16)

    high, low = split(lhs_ref[...])
    lead = rhs_ref[:, : 2 * wide]
    total = lax.dot_general(high, lead, NN, preferred_element_type=f32)
    total += lax.dot_general(low, lead, NN, preferred_element_type=f32)
    total += lax.dot_general(high, rhs_ref[:, 2 * wide :], NN, preferred_element_type=f32)
    real = total[:band, :wide] + total[band:, wide:]
    imag = total[:band, wide:] - total[band:, :wide]

    factor = 1.0 / (SPAN**3 * scale)
    column = window % readout
    for part, values in enumerate((real, imag)):
        folded = jnp.zeros((cell, wide), f32)
        for e in range(SPAN):
            moved = values[e * cell : (e + 1) * cell]
            if e != HALF:
                moved = pltpu.roll(moved, (e - HALF) % wide, 1)
            near = column - e + HALF
            folded += jnp.where((near >= 0) & (near < readout), moved, 0.0)
        folded = folded * factor
        for line in range(rows):
            for f in range(frames):
                kept = measured_ref[part, :, line, f, :]
                at = (slice(f * coils, (f + 1) * coils), slice(line * readout, (line + 1) * readout))
                out_ref[part, :, line, f, :] = jnp.where(hit_ref[at] > 0, kept, folded[at])


def pack(lines_ref, estimate_ref, packed_ref, hit_ref):
    _, coils, rows, frames, readout = estimate_ref.shape
    shape = hit_ref.shape
    line = lax.axis_index("slab") * rows + lax.broadcasted_iota(jnp.int32, shape, 1) // readout
    frame = lax.broadcasted_iota(jnp.int32, shape, 0) // coils
    hit = jnp.zeros(shape, jnp.int32)
    for f in range(frames):
        for sample in range(lines_ref.shape[1]):
            hit = jnp.where((line == lines_ref[f, sample]) & (frame == f), 1, hit)
    hit_ref[...] = hit
    groups = LANES // readout
    for part in range(2):
        for f in range(frames):
            for line in range(rows):
                down, right = divmod((part * frames + f) * rows + line, groups)
                at = (slice(down * coils, (down + 1) * coils), slice(right * readout, (right + 1) * readout))
                packed_ref[at] = estimate_ref[part, :, line, f, :]


def steps(slabs):
    stride, found = slabs, []
    while stride > 1:
        size = next(p for p in range(2, stride + 1) if stride % p == 0)
        stride //= size
        found.append((size, stride))
    return found


def place(block, slabs):
    spot, weight = 0, 1
    for size, stride in steps(slabs):
        spot += block // stride % size * weight
        weight *= size
    return spot


def gather(block):
    slabs = lax.axis_size("slab")
    held = block[None]
    for size, stride in steps(slabs):
        firsts = [i for i in range(slabs) if i // stride % size == 0]
        groups = [[i + j * stride for j in range(size)] for i in firsts]
        held = lax.all_gather(held, "slab", axis_index_groups=groups, tiled=True)
    return held


def local(estimate, measured, sampled_lines):
    _, coils, frames, rows, readout = estimate.shape
    slabs = lax.axis_size("slab")
    cell = coils * frames
    width = rows * readout
    band = SPAN * cell
    pad = up(band, LANES)
    wide = up(width, LANES)
    groups = LANES // readout
    tiles = up(slabs * rows, groups) // groups
    reach = up(LAGS, rows) // rows
    slots = 2 * SPAN - 1 + 8

    vmem = pl.BlockSpec(memory_space=pltpu.VMEM)
    packed, hit = pl.pallas_call(
        pack,
        out_shape=(
            jax.ShapeDtypeStruct((up(2 * frames * rows, groups) // groups * coils, LANES), jnp.float32),
            jax.ShapeDtypeStruct((cell, wide), jnp.int32),
        ),
        in_specs=[pl.BlockSpec(memory_space=pltpu.SMEM), vmem],
        out_specs=(vmem, vmem),
        compiler_params=pltpu.CompilerParams(vmem_limit_bytes=56 * 1024 * 1024),
        name="pack",
    )(sampled_lines, jnp.swapaxes(estimate, 2, 3))
    gathered = gather(packed)
    sizes = (slabs, coils, frames, rows, readout)
    result = pl.pallas_call(
        functools.partial(kernel, sizes),
        out_shape=jax.ShapeDtypeStruct((2, coils, rows, frames, readout), jnp.float32),
        in_specs=[vmem, vmem, vmem],
        out_specs=vmem,
        scratch_shapes=[
            pltpu.VMEM((2 * cell, (LAGS + tiles) * LANES), jnp.float32),
            pltpu.VMEM((4 * band, (LAGS + tiles) * LANES), jnp.bfloat16),
            pltpu.VMEM((4 * pad, tiles * LANES), jnp.bfloat16),
            pltpu.VMEM((2 * cell, LANES), jnp.float32),
            pltpu.VMEM((2 * cell, up((2 * reach + 1) * width + LANES, LANES)), jnp.float32),
            pltpu.VMEM((2 * band, slots * pad), jnp.float32),
            pltpu.VMEM((slots * pad, 4 * wide), jnp.bfloat16),
        ],
        compiler_params=pltpu.CompilerParams(vmem_limit_bytes=40 * 1024 * 1024),
        name="filter_step",
    )(hit, gathered, jnp.swapaxes(measured, 2, 3))
    return jnp.swapaxes(result, 2, 3)


def solution(mesh):
    placed = (
        P(None, None, "grp", "slab", None),
        P(None, None, "grp", "slab", None),
        P("grp", None),
    )
    return jax.shard_map(
        local,
        mesh=mesh,
        in_specs=placed,
        out_specs=P(None, None, "grp", "slab", None),
        check_vma=False,
    )
```

```python
import functools

import jax
import jax.numpy as jnp
from jax import lax
from jax.experimental import pallas as pl
from jax.experimental.pallas import tpu as pltpu
from jax.sharding import PartitionSpec as P

SPAN = 5
HALF = SPAN // 2
LAGS = SPAN - 1
LANES = 128
NT = (((1,), (1,)), ((), ()))
NN = (((1,), (0,)), ((), ()))


def up(size, unit):
    return -(-size // unit) * unit


def split(value):
    high = value.astype(jnp.bfloat16)
    return high, (value - high.astype(jnp.float32)).astype(jnp.bfloat16)


def repeat(count, body):
    if count <= 16:
        for step in range(count):
            body(step)
    else:
        lax.fori_loop(0, count, lambda step, carry: (body(step), carry)[1], 0)


def lane_tile(tile):
    start = tile * LANES
    return start if isinstance(start, int) else pl.multiple_of(start, LANES)


def kernel(sizes, hit_ref, gathered_ref, measured_ref, out_ref, x_ref, z_ref, zc_ref, acc_ref, xw_ref, lhs_ref, rhs_ref):
    slabs, coils, frames, rows, readout = sizes
    me = lax.axis_index("slab")
    cell = coils * frames
    band = SPAN * cell
    width = rows * readout
    groups = LANES // readout
    lines = slabs * rows
    tiles = up(lines, groups) // groups
    f32 = jnp.float32

    planes = 2 * frames

    def unpacked(block, plane, line):
        down, right = divmod(plane * rows + line, groups)
        return gathered_ref[place(block, slabs), down * coils : (down + 1) * coils, right * readout : (right + 1) * readout]

    if tiles * groups != lines:
        x_ref[...] = jnp.zeros_like(x_ref)
    for line in range(lines):
        block, inner = divmod(line, rows)
        group, tile = divmod(line, tiles)
        start = (LAGS + tile) * LANES + group * readout
        for plane in range(planes):
            x_ref[plane * coils : (plane + 1) * coils, start : start + readout] = unpacked(block, plane, inner)
    lane = lax.broadcasted_iota(jnp.int32, (2 * cell, LANES), 1)
    for back in range(1, LAGS + 1):
        source = (LAGS + tiles - back) * LANES
        wrapped = pltpu.roll(x_ref[:, source : source + LANES], readout, 1)
        target = (LAGS - back) * LANES
        x_ref[:, target : target + LANES] = jnp.where(lane >= readout, wrapped, 0.0)

    column = lane % readout
    inside = [(column + e - HALF >= 0) & (column + e - HALF < readout) for e in range(SPAN)]

    def patches(tile):
        at = pl.ds(lane_tile(tile), LANES)
        cells = x_ref[:, at]
        for e in range(SPAN):
            moved = cells if e == HALF else pltpu.roll(cells, (HALF - e) % LANES, 1)
            high, low = split(jnp.where(inside[e], moved, 0.0))
            for part in range(2):
                first = part * band + e * cell
                z_ref[first : first + cell, at] = high[part * cell : (part + 1) * cell]
                z_ref[2 * band + first : 2 * band + first + cell, at] = low[part * cell : (part + 1) * cell]

    repeat(LAGS + tiles, patches)

    pad = up(band, LANES)

    def centre(tile):
        source = pl.ds(lane_tile(tile + LAGS), LANES)
        at = pl.ds(lane_tile(tile), LANES)
        for piece in range(4):
            first = piece * pad
            zc_ref[first : first + band, at] = z_ref[piece * band : (piece + 1) * band, source]
            zc_ref[first + band : first + pad, at] = jnp.zeros((pad - band, LANES), jnp.bfloat16)

    repeat(tiles, centre)

    line_base = lane // readout * tiles
    acc_ref[...] = jnp.zeros_like(acc_ref)

    def energy(tile):
        cells = x_ref[:, pl.ds(lane_tile(tile + LAGS), LANES)]
        line = line_base + tile
        covers = jnp.minimum(line + HALF, lines - 1) - jnp.maximum(line - HALF, 0) + 1
        acc_ref[...] += cells * cells * covers.astype(f32)

    repeat(tiles, energy)
    row = lax.broadcasted_iota(jnp.int32, (2 * cell, LANES), 0)
    frame = row // coils % frames
    covers_t = jnp.minimum(frame + HALF, frames - 1) - jnp.maximum(frame - HALF, 0) + 1
    covers_x = jnp.minimum(column + HALF, readout - 1) - jnp.maximum(column - HALF, 0) + 1
    weighted = acc_ref[...] * (covers_t * covers_x).astype(f32)
    trace = jnp.sum(jnp.sum(weighted, axis=1, keepdims=True), axis=0, keepdims=True)
    scale = trace / (SPAN**3 * coils) + 1e-06

    def product(left, right):
        both = lax.dot_general(left, right[: 2 * pad], NT, preferred_element_type=f32)
        cross = lax.dot_general(left[: 2 * band], right[2 * pad :], NT, preferred_element_type=f32)
        return both[: 2 * band] + both[2 * band :] + cross

    mrow = lax.broadcasted_iota(jnp.int32, (band, pad), 0) // coils % frames
    mcol = lax.broadcasted_iota(jnp.int32, (band, pad), 1) // coils % frames
    mixes = []
    for shift in range(-frames + 1, frames):
        mask = jnp.zeros((band, pad), f32)
        for i in range(frames):
            for j in range(frames):
                if 0 <= i + shift < frames and 0 <= j + shift < frames:
                    count = sum(
                        abs(i - t) <= HALF and abs(j - t) <= HALF and 0 <= t + shift < frames for t in range(frames)
                    )
                    mask = jnp.where((mrow == i) & (mcol == j), float(count), mask)
        mixes.append((shift, mask))

    def mixed(gram):
        total = None
        for shift, mask in mixes:
            moved = gram
            if shift:
                moved = pltpu.roll(pltpu.roll(gram, -shift * coils % pad, 1), -shift * coils % band, 0)
            total = moved * mask if total is None else total + moved * mask
        return total

    def complex_gram(stacked):
        real = stacked[:band, :pad] + stacked[band:, pad:]
        imag = stacked[:band, pad:] - stacked[band:, :pad]
        return mixed(real), mixed(imag)

    slot = 0
    order = []

    def put(real, imag, lag, weight):
        nonlocal slot
        lhs_ref[:band, slot * pad : (slot + 1) * pad] = real
        lhs_ref[band:, slot * pad : (slot + 1) * pad] = imag
        order.append((lag, weight))
        slot += 1

    def put_both(pair, lag, weight, back_weight):
        real, imag = pair
        put(real, imag, lag, weight)
        fill = jnp.zeros((pad - band, pad), f32)
        real_t = jnp.transpose(jnp.concatenate([real, fill], axis=0))[:band]
        imag_t = jnp.transpose(jnp.concatenate([imag, fill], axis=0))[:band]
        put(real_t, -imag_t, -lag, back_weight)

    window = lax.broadcasted_iota(jnp.int32, (cell, up(width, LANES)), 1)
    my_line = me * rows + window // readout
    valid = [((my_line - b + HALF >= 0) & (my_line - b + HALF < lines)).astype(f32) for b in range(SPAN)]

    def lag_weight(lag):
        total = None
        for b in range(SPAN):
            if 0 <= b + lag < SPAN:
                total = valid[b] if total is None else total + valid[b]
        return total

    depth = max(d for d in range(1, 17) if tiles % d == 0)
    for lag in range(SPAN):

        def part(step):
            left = z_ref[:, pl.ds(lane_tile(LAGS - lag + step * depth), depth * LANES)]
            right = zc_ref[:, pl.ds(lane_tile(step * depth), depth * LANES)]
            return product(left, right)

        if tiles == depth:
            stacked = part(0)
        else:
            stacked = lax.fori_loop(
                0, tiles // depth, lambda step, total: total + part(step), jnp.zeros((2 * band, 2 * pad), f32)
            )
        pair = complex_gram(stacked)
        if lag == 0:
            put(*pair, 0, lag_weight(0))
        else:
            put_both(pair, lag, lag_weight(lag), lag_weight(-lag))

    def edge(first, second):
        group, tile = divmod(first, tiles)
        other = second % tiles
        start = (LAGS + tile) * LANES
        here = lax.broadcasted_iota(jnp.int32, (4 * band, LANES), 1) // readout == group
        left = jnp.where(here, z_ref[:, start : start + LANES].astype(f32), 0.0).astype(jnp.bfloat16)
        return complex_gram(product(left, zc_ref[:, other * LANES : (other + 1) * LANES]))

    last = lines - 1
    put(*edge(last - 1, last - 1), 0, -valid[0])
    put(*edge(last, last), 0, -(valid[0] + valid[1]))
    put(*edge(0, 0), 0, -(valid[3] + valid[4]))
    put(*edge(1, 1), 0, -valid[4])
    put_both(edge(last - 1, last), 1, -valid[0], -valid[1])
    put_both(edge(0, 1), 1, -valid[3], -valid[4])

    reach = up(LAGS, rows) // rows
    for j in range(-reach, reach + 1):
        block = me + j
        exists = (block >= 0) & (block < slabs)
        block = jnp.clip(block, 0, slabs - 1)
        for line in range(rows):
            start = (j + reach) * width + line * readout
            for plane in range(planes):
                held = jnp.where(exists, unpacked(block, plane, line), 0.0)
                xw_ref[plane * coils : (plane + 1) * coils, start : start + readout] = held
    extent = xw_ref.shape[1]
    spread = lax.broadcasted_iota(jnp.int32, (2 * cell, extent), 1) % readout
    around = xw_ref[...]
    wide = up(width, LANES)
    for e in range(SPAN):
        moved = around if e == HALF else pltpu.roll(around, (HALF - e) % extent, 1)
        near = spread + e - HALF
        moved = jnp.where((near >= 0) & (near < readout), moved, 0.0)
        for lag in range(-LAGS, LAGS + 1):
            start = (reach * rows + lag) * readout
            piece = moved[:, start : start + wide]
            for index, (at, weight) in enumerate(order):
                if at == lag:
                    first = index * pad + e * cell
                    for part in range(2):
                        high, low = split(piece[part * cell : (part + 1) * cell] * weight)
                        rhs_ref[first : first + cell, part * wide : (part + 1) * wide] = high
                        rhs_ref[first : first + cell, (2 + part) * wide : (3 + part) * wide] = low
    for index in range(len(order)):
        first = index * pad
        rhs_ref[first + band : first + pad, :] = jnp.zeros((pad - band, 4 * wide), jnp.bfloat16)

    high, low = split(lhs_ref[...])
    lead = rhs_ref[:, : 2 * wide]
    total = lax.dot_general(high, lead, NN, preferred_element_type=f32)
    total += lax.dot_general(low, lead, NN, preferred_element_type=f32)
    total += lax.dot_general(high, rhs_ref[:, 2 * wide :], NN, preferred_element_type=f32)
    real = total[:band, :wide] + total[band:, wide:]
    imag = total[:band, wide:] - total[band:, :wide]

    factor = 1.0 / (SPAN**3 * scale)
    column = window % readout
    for part, values in enumerate((real, imag)):
        folded = jnp.zeros((cell, wide), f32)
        for e in range(SPAN):
            moved = values[e * cell : (e + 1) * cell]
            if e != HALF:
                moved = pltpu.roll(moved, (e - HALF) % wide, 1)
            near = column - e + HALF
            folded += jnp.where((near >= 0) & (near < readout), moved, 0.0)
        folded = folded * factor
        for line in range(rows):
            for f in range(frames):
                kept = measured_ref[part, :, line, f, :]
                at = (slice(f * coils, (f + 1) * coils), slice(line * readout, (line + 1) * readout))
                out_ref[part, :, line, f, :] = jnp.where(hit_ref[at] > 0, kept, folded[at])


def pack(lines_ref, estimate_ref, packed_ref, hit_ref):
    _, coils, rows, frames, readout = estimate_ref.shape
    shape = hit_ref.shape
    line = lax.axis_index("slab") * rows + lax.broadcasted_iota(jnp.int32, shape, 1) // readout
    frame = lax.broadcasted_iota(jnp.int32, shape, 0) // coils
    hit = jnp.zeros(shape, jnp.int32)
    for f in range(frames):
        for sample in range(lines_ref.shape[1]):
            hit = jnp.where((line == lines_ref[f, sample]) & (frame == f), 1, hit)
    hit_ref[...] = hit
    groups = LANES // readout
    for part in range(2):
        for f in range(frames):
            for line in range(rows):
                down, right = divmod((part * frames + f) * rows + line, groups)
                at = (0, slice(down * coils, (down + 1) * coils), slice(right * readout, (right + 1) * readout))
                packed_ref[at] = estimate_ref[part, :, line, f, :]
    packed = packed_ref[0]
    for copy in range(1, packed_ref.shape[0]):
        packed_ref[copy] = packed


def nearby(slabs):
    return 2 if slabs % 2 == 0 else 1


def place(block, slabs):
    near = nearby(slabs)
    return block % near * (slabs // near) + block // near


def gather(copies, slabs):
    near, far = nearby(slabs), slabs // nearby(slabs)
    alike = [[i + j * near for j in range(far)] for i in range(near)]
    chips = [[i * near + j for j in range(near)] for i in range(far)]
    half = lax.all_to_all(copies, "slab", 0, 0, axis_index_groups=alike)
    return lax.all_gather(half, "slab", axis_index_groups=chips, tiled=True)


def local(estimate, measured, sampled_lines):
    _, coils, frames, rows, readout = estimate.shape
    slabs = lax.axis_size("slab")
    cell = coils * frames
    width = rows * readout
    band = SPAN * cell
    pad = up(band, LANES)
    wide = up(width, LANES)
    groups = LANES // readout
    tiles = up(slabs * rows, groups) // groups
    reach = up(LAGS, rows) // rows
    slots = 2 * SPAN - 1 + 8

    vmem = pl.BlockSpec(memory_space=pltpu.VMEM)
    copies = slabs // nearby(slabs)
    packed, hit = pl.pallas_call(
        pack,
        out_shape=(
            jax.ShapeDtypeStruct((copies, up(2 * frames * rows, groups) // groups * coils, LANES), jnp.float32),
            jax.ShapeDtypeStruct((cell, wide), jnp.int32),
        ),
        in_specs=[pl.BlockSpec(memory_space=pltpu.SMEM), vmem],
        out_specs=(vmem, vmem),
        compiler_params=pltpu.CompilerParams(vmem_limit_bytes=56 * 1024 * 1024),
        name="pack",
    )(sampled_lines, jnp.swapaxes(estimate, 2, 3))
    gathered = gather(packed, slabs)
    sizes = (slabs, coils, frames, rows, readout)
    result = pl.pallas_call(
        functools.partial(kernel, sizes),
        out_shape=jax.ShapeDtypeStruct((2, coils, rows, frames, readout), jnp.float32),
        in_specs=[vmem, vmem, vmem],
        out_specs=vmem,
        scratch_shapes=[
            pltpu.VMEM((2 * cell, (LAGS + tiles) * LANES), jnp.float32),
            pltpu.VMEM((4 * band, (LAGS + tiles) * LANES), jnp.bfloat16),
            pltpu.VMEM((4 * pad, tiles * LANES), jnp.bfloat16),
            pltpu.VMEM((2 * cell, LANES), jnp.float32),
            pltpu.VMEM((2 * cell, up((2 * reach + 1) * width + LANES, LANES)), jnp.float32),
            pltpu.VMEM((2 * band, slots * pad), jnp.float32),
            pltpu.VMEM((slots * pad, 4 * wide), jnp.bfloat16),
        ],
        compiler_params=pltpu.CompilerParams(vmem_limit_bytes=40 * 1024 * 1024),
        name="filter_step",
    )(hit, gathered, jnp.swapaxes(measured, 2, 3))
    return jnp.swapaxes(result, 2, 3)


def solution(mesh):
    placed = (
        P(None, None, "grp", "slab", None),
        P(None, None, "grp", "slab", None),
        P("grp", None),
    )
    return jax.shard_map(
        local,
        mesh=mesh,
        in_specs=placed,
        out_specs=P(None, None, "grp", "slab", None),
        check_vma=False,
    )
```

```python
import functools

import jax
import jax.numpy as jnp
from jax import lax
from jax.experimental import pallas as pl
from jax.experimental.pallas import tpu as pltpu
from jax.sharding import PartitionSpec as P

SPAN = 5
HALF = SPAN // 2
LAGS = SPAN - 1
LANES = 128
NT = (((1,), (1,)), ((), ()))
NN = (((1,), (0,)), ((), ()))


def up(size, unit):
    return -(-size // unit) * unit


def split(value):
    high = value.astype(jnp.bfloat16)
    return high, (value - high.astype(jnp.float32)).astype(jnp.bfloat16)


def repeat(count, body):
    if count <= 16:
        for step in range(count):
            body(step)
    else:
        lax.fori_loop(0, count, lambda step, carry: (body(step), carry)[1], 0)


def lane_tile(tile):
    start = tile * LANES
    return start if isinstance(start, int) else pl.multiple_of(start, LANES)


def kernel(sizes, hit_ref, gathered_ref, measured_ref, out_ref, x_ref, z_ref, zc_ref, acc_ref, xw_ref, lhs_ref, rhs_ref):
    slabs, coils, frames, rows, readout = sizes
    me = lax.axis_index("slab")
    cell = coils * frames
    band = SPAN * cell
    pad = up(band, LANES)
    width = rows * readout
    groups = LANES // readout
    lines = slabs * rows
    tiles = up(lines, groups) // groups
    f32 = jnp.float32

    planes = 2 * frames

    def unpacked(block, plane, line):
        down, right = divmod(plane * rows + line, groups)
        return gathered_ref[block, down * coils : (down + 1) * coils, right * readout : (right + 1) * readout]

    if tiles * groups != lines:
        x_ref[...] = jnp.zeros_like(x_ref)
    for line in range(lines):
        block, inner = divmod(line, rows)
        group, tile = divmod(line, tiles)
        start = (LAGS + tile) * LANES + group * readout
        for plane in range(planes):
            x_ref[plane * coils : (plane + 1) * coils, start : start + readout] = unpacked(block, plane, inner)
    lane = lax.broadcasted_iota(jnp.int32, (2 * cell, LANES), 1)
    for back in range(1, LAGS + 1):
        source = (LAGS + tiles - back) * LANES
        wrapped = pltpu.roll(x_ref[:, source : source + LANES], readout, 1)
        target = (LAGS - back) * LANES
        x_ref[:, target : target + LANES] = jnp.where(lane >= readout, wrapped, 0.0)

    column = lane % readout
    inside = [(column + e - HALF >= 0) & (column + e - HALF < readout) for e in range(SPAN)]

    stacked = stacks(tiles)
    held = SPAN if stacked else 1

    def patches(tile):
        source = pl.ds(lane_tile(tile), LANES)
        if stacked:
            targets = [(lag, tile - LAGS + lag) for lag in range(SPAN) if 0 <= tile - LAGS + lag < tiles]
        else:
            targets = [(0, tile)]
        cells = x_ref[:, source]
        for e in range(SPAN):
            moved = cells if e == HALF else pltpu.roll(cells, (HALF - e) % LANES, 1)
            high, low = split(jnp.where(inside[e], moved, 0.0))
            for lag, target in targets:
                at = pl.ds(lane_tile(target), LANES)
                for part in range(2):
                    first = (2 * lag + part) * band + e * cell
                    z_ref[first : first + cell, at] = high[part * cell : (part + 1) * cell]
                    first += 2 * held * band
                    z_ref[first : first + cell, at] = low[part * cell : (part + 1) * cell]
            if stacked and tile >= LAGS:
                at = pl.ds(lane_tile(tile - LAGS), LANES)
                for part in range(2):
                    first = part * pad + e * cell
                    zc_ref[first : first + cell, at] = high[part * cell : (part + 1) * cell]
                    first += 2 * pad
                    zc_ref[first : first + cell, at] = low[part * cell : (part + 1) * cell]

    if stacked:
        for tile in range(LAGS + tiles):
            patches(tile)
    else:
        repeat(LAGS + tiles, patches)

    def centre(tile):
        source = pl.ds(lane_tile(tile + LAGS), LANES)
        at = pl.ds(lane_tile(tile), LANES)
        for piece in range(4):
            first = piece * pad
            if not stacked:
                zc_ref[first : first + band, at] = z_ref[piece * band : (piece + 1) * band, source]
            zc_ref[first + band : first + pad, at] = jnp.zeros((pad - band, LANES), jnp.bfloat16)

    repeat(tiles, centre)

    line_base = lane // readout * tiles
    acc_ref[...] = jnp.zeros_like(acc_ref)

    def energy(tile):
        cells = x_ref[:, pl.ds(lane_tile(tile + LAGS), LANES)]
        line = line_base + tile
        covers = jnp.minimum(line + HALF, lines - 1) - jnp.maximum(line - HALF, 0) + 1
        acc_ref[...] += cells * cells * covers.astype(f32)

    repeat(tiles, energy)
    row = lax.broadcasted_iota(jnp.int32, (2 * cell, LANES), 0)
    frame = row // coils % frames
    covers_t = jnp.minimum(frame + HALF, frames - 1) - jnp.maximum(frame - HALF, 0) + 1
    covers_x = jnp.minimum(column + HALF, readout - 1) - jnp.maximum(column - HALF, 0) + 1
    weighted = acc_ref[...] * (covers_t * covers_x).astype(f32)
    trace = jnp.sum(jnp.sum(weighted, axis=1, keepdims=True), axis=0, keepdims=True)
    scale = trace / (SPAN**3 * coils) + 1e-06

    def product(left, right):
        half = left.shape[0] // 2
        both = lax.dot_general(left, right[: 2 * pad], NT, preferred_element_type=f32)
        cross = lax.dot_general(left[:half], right[2 * pad :], NT, preferred_element_type=f32)
        return both[:half] + both[half:] + cross

    mrow = lax.broadcasted_iota(jnp.int32, (band, pad), 0) // coils % frames
    mcol = lax.broadcasted_iota(jnp.int32, (band, pad), 1) // coils % frames
    mixes = []
    for shift in range(-frames + 1, frames):
        mask = jnp.zeros((band, pad), f32)
        for i in range(frames):
            for j in range(frames):
                if 0 <= i + shift < frames and 0 <= j + shift < frames:
                    count = sum(
                        abs(i - t) <= HALF and abs(j - t) <= HALF and 0 <= t + shift < frames for t in range(frames)
                    )
                    mask = jnp.where((mrow == i) & (mcol == j), float(count), mask)
        mixes.append((shift, mask))

    def mixed(gram):
        total = None
        for shift, mask in mixes:
            moved = gram
            if shift:
                moved = pltpu.roll(pltpu.roll(gram, -shift * coils % pad, 1), -shift * coils % band, 0)
            total = moved * mask if total is None else total + moved * mask
        return total

    def complex_gram(sums):
        real = sums[:band, :pad] + sums[band:, pad:]
        imag = sums[:band, pad:] - sums[band:, :pad]
        return mixed(real), mixed(imag)

    slot = 0
    order = []

    def put(real, imag, lag, weight):
        nonlocal slot
        lhs_ref[:band, slot * pad : (slot + 1) * pad] = real
        lhs_ref[band:, slot * pad : (slot + 1) * pad] = imag
        order.append((lag, weight))
        slot += 1

    def put_both(pair, lag, weight, back_weight):
        real, imag = pair
        put(real, imag, lag, weight)
        fill = jnp.zeros((pad - band, pad), f32)
        real_t = jnp.transpose(jnp.concatenate([real, fill], axis=0))[:band]
        imag_t = jnp.transpose(jnp.concatenate([imag, fill], axis=0))[:band]
        put(real_t, -imag_t, -lag, back_weight)

    window = lax.broadcasted_iota(jnp.int32, (cell, up(width, LANES)), 1)
    my_line = me * rows + window // readout
    valid = [((my_line - b + HALF >= 0) & (my_line - b + HALF < lines)).astype(f32) for b in range(SPAN)]

    def lag_weight(lag):
        total = None
        for b in range(SPAN):
            if 0 <= b + lag < SPAN:
                total = valid[b] if total is None else total + valid[b]
        return total

    if stacked:
        every = product(z_ref[...], zc_ref[...])
    depth = max(d for d in range(1, 17) if tiles % d == 0)
    for lag in range(SPAN):

        def part(step):
            left = z_ref[:, pl.ds(lane_tile(LAGS - lag + step * depth), depth * LANES)]
            right = zc_ref[:, pl.ds(lane_tile(step * depth), depth * LANES)]
            return product(left, right)

        if stacked:
            sums = every[2 * band * lag : 2 * band * (lag + 1)]
        else:
            sums = lax.fori_loop(
                0, tiles // depth, lambda step, total: total + part(step), jnp.zeros((2 * band, 2 * pad), f32)
            )
        pair = complex_gram(sums)
        if lag == 0:
            put(*pair, 0, lag_weight(0))
        else:
            put_both(pair, lag, lag_weight(lag), lag_weight(-lag))

    def edge(first, second):
        group, tile = divmod(first, tiles)
        other = second % tiles
        start = tile * LANES if stacked else (LAGS + tile) * LANES
        here = lax.broadcasted_iota(jnp.int32, (2 * band, LANES), 1) // readout == group
        halves = []
        for base in (0, 2 * held * band):
            value = z_ref[base : base + 2 * band, start : start + LANES].astype(f32)
            halves.append(jnp.where(here, value, 0.0).astype(jnp.bfloat16))
        left = jnp.concatenate(halves, axis=0)
        return complex_gram(product(left, zc_ref[:, other * LANES : (other + 1) * LANES]))

    last = lines - 1
    put(*edge(last - 1, last - 1), 0, -valid[0])
    put(*edge(last, last), 0, -(valid[0] + valid[1]))
    put(*edge(0, 0), 0, -(valid[3] + valid[4]))
    put(*edge(1, 1), 0, -valid[4])
    put_both(edge(last - 1, last), 1, -valid[0], -valid[1])
    put_both(edge(0, 1), 1, -valid[3], -valid[4])

    reach = up(LAGS, rows) // rows
    for j in range(-reach, reach + 1):
        block = me + j
        exists = (block >= 0) & (block < slabs)
        block = jnp.clip(block, 0, slabs - 1)
        for line in range(rows):
            start = (j + reach) * width + line * readout
            for plane in range(planes):
                held = jnp.where(exists, unpacked(block, plane, line), 0.0)
                xw_ref[plane * coils : (plane + 1) * coils, start : start + readout] = held
    extent = xw_ref.shape[1]
    spread = lax.broadcasted_iota(jnp.int32, (2 * cell, extent), 1) % readout
    around = xw_ref[...]
    wide = up(width, LANES)
    for e in range(SPAN):
        moved = around if e == HALF else pltpu.roll(around, (HALF - e) % extent, 1)
        near = spread + e - HALF
        moved = jnp.where((near >= 0) & (near < readout), moved, 0.0)
        for lag in range(-LAGS, LAGS + 1):
            start = (reach * rows + lag) * readout
            piece = moved[:, start : start + wide]
            for index, (at, weight) in enumerate(order):
                if at == lag:
                    first = index * pad + e * cell
                    for part in range(2):
                        high, low = split(piece[part * cell : (part + 1) * cell] * weight)
                        rhs_ref[first : first + cell, part * wide : (part + 1) * wide] = high
                        rhs_ref[first : first + cell, (2 + part) * wide : (3 + part) * wide] = low
    for index in range(len(order)):
        first = index * pad
        rhs_ref[first + band : first + pad, :] = jnp.zeros((pad - band, 4 * wide), jnp.bfloat16)

    high, low = split(lhs_ref[...])
    lead = rhs_ref[:, : 2 * wide]
    total = lax.dot_general(high, lead, NN, preferred_element_type=f32)
    total += lax.dot_general(low, lead, NN, preferred_element_type=f32)
    total += lax.dot_general(high, rhs_ref[:, 2 * wide :], NN, preferred_element_type=f32)
    real = total[:band, :wide] + total[band:, wide:]
    imag = total[:band, wide:] - total[band:, :wide]

    factor = 1.0 / (SPAN**3 * scale)
    column = window % readout
    for part, values in enumerate((real, imag)):
        folded = jnp.zeros((cell, wide), f32)
        for e in range(SPAN):
            moved = values[e * cell : (e + 1) * cell]
            if e != HALF:
                moved = pltpu.roll(moved, (e - HALF) % wide, 1)
            near = column - e + HALF
            folded += jnp.where((near >= 0) & (near < readout), moved, 0.0)
        folded = folded * factor
        for line in range(rows):
            for f in range(frames):
                kept = measured_ref[part, :, line, f, :]
                at = (slice(f * coils, (f + 1) * coils), slice(line * readout, (line + 1) * readout))
                out_ref[part, :, line, f, :] = jnp.where(hit_ref[at] > 0, kept, folded[at])


def pack(lines_ref, estimate_ref, packed_ref, hit_ref):
    _, coils, rows, frames, readout = estimate_ref.shape
    shape = hit_ref.shape
    line = lax.axis_index("slab") * rows + lax.broadcasted_iota(jnp.int32, shape, 1) // readout
    frame = lax.broadcasted_iota(jnp.int32, shape, 0) // coils
    hit = jnp.zeros(shape, jnp.int32)
    for f in range(frames):
        for sample in range(lines_ref.shape[1]):
            hit = jnp.where((line == lines_ref[f, sample]) & (frame == f), 1, hit)
    hit_ref[...] = hit
    groups = LANES // readout
    for part in range(2):
        for f in range(frames):
            for line in range(rows):
                down, right = divmod((part * frames + f) * rows + line, groups)
                at = (0, slice(down * coils, (down + 1) * coils), slice(right * readout, (right + 1) * readout))
                packed_ref[at] = estimate_ref[part, :, line, f, :]
    packed = packed_ref[0]
    for copy in range(1, packed_ref.shape[0]):
        packed_ref[copy] = packed


def gather(copies):
    return lax.all_to_all(copies, "slab", 0, 0)


def stacks(tiles):
    return tiles <= 16


def local(estimate, measured, sampled_lines):
    _, coils, frames, rows, readout = estimate.shape
    slabs = lax.axis_size("slab")
    cell = coils * frames
    width = rows * readout
    band = SPAN * cell
    pad = up(band, LANES)
    wide = up(width, LANES)
    groups = LANES // readout
    tiles = up(slabs * rows, groups) // groups
    reach = up(LAGS, rows) // rows
    slots = 2 * SPAN - 1 + 8
    columns = (tiles if stacks(tiles) else LAGS + tiles) * LANES

    vmem = pl.BlockSpec(memory_space=pltpu.VMEM)
    packed, hit = pl.pallas_call(
        pack,
        out_shape=(
            jax.ShapeDtypeStruct((slabs, up(2 * frames * rows, groups) // groups * coils, LANES), jnp.float32),
            jax.ShapeDtypeStruct((cell, wide), jnp.int32),
        ),
        in_specs=[pl.BlockSpec(memory_space=pltpu.SMEM), vmem],
        out_specs=(vmem, vmem),
        compiler_params=pltpu.CompilerParams(vmem_limit_bytes=56 * 1024 * 1024),
        name="pack",
    )(sampled_lines, jnp.swapaxes(estimate, 2, 3))
    gathered = gather(packed)
    sizes = (slabs, coils, frames, rows, readout)
    result = pl.pallas_call(
        functools.partial(kernel, sizes),
        out_shape=jax.ShapeDtypeStruct((2, coils, rows, frames, readout), jnp.float32),
        in_specs=[vmem, vmem, vmem],
        out_specs=vmem,
        scratch_shapes=[
            pltpu.VMEM((2 * cell, (LAGS + tiles) * LANES), jnp.float32),
            pltpu.VMEM((4 * band * (SPAN if stacks(tiles) else 1), columns), jnp.bfloat16),
            pltpu.VMEM((4 * pad, tiles * LANES), jnp.bfloat16),
            pltpu.VMEM((2 * cell, LANES), jnp.float32),
            pltpu.VMEM((2 * cell, up((2 * reach + 1) * width + LANES, LANES)), jnp.float32),
            pltpu.VMEM((2 * band, slots * pad), jnp.float32),
            pltpu.VMEM((slots * pad, 4 * wide), jnp.bfloat16),
        ],
        compiler_params=pltpu.CompilerParams(vmem_limit_bytes=40 * 1024 * 1024),
        name="filter_step",
    )(hit, gathered, jnp.swapaxes(measured, 2, 3))
    return jnp.swapaxes(result, 2, 3)


def solution(mesh):
    placed = (
        P(None, None, "grp", "slab", None),
        P(None, None, "grp", "slab", None),
        P("grp", None),
    )
    return jax.shard_map(
        local,
        mesh=mesh,
        in_specs=placed,
        out_specs=P(None, None, "grp", "slab", None),
        check_vma=False,
    )
```

```python
import functools

import jax
import jax.numpy as jnp
from jax import lax
from jax.experimental import pallas as pl
from jax.experimental.pallas import tpu as pltpu
from jax.sharding import PartitionSpec as P

SPAN = 5
HALF = SPAN // 2
LAGS = SPAN - 1
LANES = 128
NT = (((1,), (1,)), ((), ()))
NN = (((1,), (0,)), ((), ()))


def up(size, unit):
    return -(-size // unit) * unit


def split(value):
    high = value.astype(jnp.bfloat16)
    return high, (value - high.astype(jnp.float32)).astype(jnp.bfloat16)


def repeat(count, body):
    if count <= 16:
        for step in range(count):
            body(step)
    else:
        lax.fori_loop(0, count, lambda step, carry: (body(step), carry)[1], 0)


def lane_tile(tile):
    start = tile * LANES
    return start if isinstance(start, int) else pl.multiple_of(start, LANES)


def kernel(sizes, hit_ref, gathered_ref, measured_ref, out_ref, x_ref, z_ref, zc_ref, acc_ref, xw_ref, lhs_ref, rhs_ref):
    slabs, coils, frames, rows, readout = sizes
    me = lax.axis_index("slab")
    cell = coils * frames
    band = SPAN * cell
    pad = up(band, LANES)
    width = rows * readout
    groups = LANES // readout
    lines = slabs * rows
    tiles = up(lines, groups) // groups
    f32 = jnp.float32

    planes = 2 * frames

    def unpacked(block, plane, line):
        down, right = divmod(plane * rows + line, groups)
        return gathered_ref[block, down * coils : (down + 1) * coils, right * readout : (right + 1) * readout]

    window = lax.broadcasted_iota(jnp.int32, (cell, up(width, LANES)), 1)
    my_line = me * rows + window // readout
    valid = [((my_line - b + HALF >= 0) & (my_line - b + HALF < lines)).astype(f32) for b in range(SPAN)]

    def lag_weight(lag):
        total = None
        for b in range(SPAN):
            if 0 <= b + lag < SPAN:
                total = valid[b] if total is None else total + valid[b]
        return total

    order = [(0, lag_weight(0))]
    for lag in range(1, SPAN):
        order += [(lag, lag_weight(lag)), (-lag, lag_weight(-lag))]
    order += [(0, -valid[0]), (0, -(valid[0] + valid[1])), (0, -(valid[3] + valid[4])), (0, -valid[4])]
    order += [(1, -valid[0]), (-1, -valid[1]), (1, -valid[3]), (-1, -valid[4])]

    reach = up(LAGS, rows) // rows
    for j in range(-reach, reach + 1):
        block = me + j
        exists = (block >= 0) & (block < slabs)
        block = jnp.clip(block, 0, slabs - 1)
        for line in range(rows):
            start = (j + reach) * width + line * readout
            for plane in range(planes):
                held = jnp.where(exists, unpacked(block, plane, line), 0.0)
                xw_ref[plane * coils : (plane + 1) * coils, start : start + readout] = held
    extent = xw_ref.shape[1]
    spread = lax.broadcasted_iota(jnp.int32, (2 * cell, extent), 1) % readout
    around = xw_ref[...]
    wide = up(width, LANES)
    for e in range(SPAN):
        moved = around if e == HALF else pltpu.roll(around, (HALF - e) % extent, 1)
        near = spread + e - HALF
        moved = jnp.where((near >= 0) & (near < readout), moved, 0.0)
        for lag in range(-LAGS, LAGS + 1):
            start = (reach * rows + lag) * readout
            piece = moved[:, start : start + wide]
            for index, (at, weight) in enumerate(order):
                if at == lag:
                    first = index * pad + e * cell
                    for part in range(2):
                        high, low = split(piece[part * cell : (part + 1) * cell] * weight)
                        rhs_ref[first : first + cell, part * wide : (part + 1) * wide] = high
                        rhs_ref[first : first + cell, (2 + part) * wide : (3 + part) * wide] = low
    for index in range(len(order)):
        first = index * pad
        rhs_ref[first + band : first + pad, :] = jnp.zeros((pad - band, 4 * wide), jnp.bfloat16)

    if tiles * groups != lines:
        x_ref[...] = jnp.zeros_like(x_ref)
    for line in range(lines):
        block, inner = divmod(line, rows)
        group, tile = divmod(line, tiles)
        start = (LAGS + tile) * LANES + group * readout
        for plane in range(planes):
            x_ref[plane * coils : (plane + 1) * coils, start : start + readout] = unpacked(block, plane, inner)
    lane = lax.broadcasted_iota(jnp.int32, (2 * cell, LANES), 1)
    for back in range(1, LAGS + 1):
        source = (LAGS + tiles - back) * LANES
        wrapped = pltpu.roll(x_ref[:, source : source + LANES], readout, 1)
        target = (LAGS - back) * LANES
        x_ref[:, target : target + LANES] = jnp.where(lane >= readout, wrapped, 0.0)

    column = lane % readout
    inside = [(column + e - HALF >= 0) & (column + e - HALF < readout) for e in range(SPAN)]

    stacked = stacks(tiles)
    held = SPAN if stacked else 1

    def patches(tile):
        source = pl.ds(lane_tile(tile), LANES)
        if stacked:
            targets = [(lag, tile - LAGS + lag) for lag in range(SPAN) if 0 <= tile - LAGS + lag < tiles]
        else:
            targets = [(0, tile)]
        cells = x_ref[:, source]
        for e in range(SPAN):
            moved = cells if e == HALF else pltpu.roll(cells, (HALF - e) % LANES, 1)
            high, low = split(jnp.where(inside[e], moved, 0.0))
            for lag, target in targets:
                at = pl.ds(lane_tile(target), LANES)
                for part in range(2):
                    first = (2 * lag + part) * band + e * cell
                    z_ref[first : first + cell, at] = high[part * cell : (part + 1) * cell]
                    first += 2 * held * band
                    z_ref[first : first + cell, at] = low[part * cell : (part + 1) * cell]
            if stacked and tile >= LAGS:
                at = pl.ds(lane_tile(tile - LAGS), LANES)
                for part in range(2):
                    first = part * pad + e * cell
                    zc_ref[first : first + cell, at] = high[part * cell : (part + 1) * cell]
                    first += 2 * pad
                    zc_ref[first : first + cell, at] = low[part * cell : (part + 1) * cell]

    if stacked:
        for tile in range(LAGS + tiles):
            patches(tile)
    else:
        repeat(LAGS + tiles, patches)

    def centre(tile):
        source = pl.ds(lane_tile(tile + LAGS), LANES)
        at = pl.ds(lane_tile(tile), LANES)
        for piece in range(4):
            first = piece * pad
            if not stacked:
                zc_ref[first : first + band, at] = z_ref[piece * band : (piece + 1) * band, source]
            zc_ref[first + band : first + pad, at] = jnp.zeros((pad - band, LANES), jnp.bfloat16)

    repeat(tiles, centre)

    line_base = lane // readout * tiles
    acc_ref[...] = jnp.zeros_like(acc_ref)

    def energy(tile):
        cells = x_ref[:, pl.ds(lane_tile(tile + LAGS), LANES)]
        line = line_base + tile
        covers = jnp.minimum(line + HALF, lines - 1) - jnp.maximum(line - HALF, 0) + 1
        acc_ref[...] += cells * cells * covers.astype(f32)

    repeat(tiles, energy)
    row = lax.broadcasted_iota(jnp.int32, (2 * cell, LANES), 0)
    frame = row // coils % frames
    covers_t = jnp.minimum(frame + HALF, frames - 1) - jnp.maximum(frame - HALF, 0) + 1
    covers_x = jnp.minimum(column + HALF, readout - 1) - jnp.maximum(column - HALF, 0) + 1
    weighted = acc_ref[...] * (covers_t * covers_x).astype(f32)
    trace = jnp.sum(jnp.sum(weighted, axis=1, keepdims=True), axis=0, keepdims=True)
    scale = trace / (SPAN**3 * coils) + 1e-06

    def product(left, right):
        half = left.shape[0] // 2
        both = lax.dot_general(left, right[: 2 * pad], NT, preferred_element_type=f32)
        cross = lax.dot_general(left[:half], right[2 * pad :], NT, preferred_element_type=f32)
        return both[:half] + both[half:] + cross

    mrow = lax.broadcasted_iota(jnp.int32, (band, pad), 0) // coils % frames
    mcol = lax.broadcasted_iota(jnp.int32, (band, pad), 1) // coils % frames
    mixes = []
    for shift in range(-frames + 1, frames):
        mask = jnp.zeros((band, pad), f32)
        for i in range(frames):
            for j in range(frames):
                if 0 <= i + shift < frames and 0 <= j + shift < frames:
                    count = sum(
                        abs(i - t) <= HALF and abs(j - t) <= HALF and 0 <= t + shift < frames for t in range(frames)
                    )
                    mask = jnp.where((mrow == i) & (mcol == j), float(count), mask)
        mixes.append((shift, mask))

    def mixed(gram):
        total = None
        for shift, mask in mixes:
            moved = gram
            if shift:
                moved = pltpu.roll(pltpu.roll(gram, -shift * coils % pad, 1), -shift * coils % band, 0)
            total = moved * mask if total is None else total + moved * mask
        return total

    def complex_gram(sums):
        real = sums[:band, :pad] + sums[band:, pad:]
        imag = sums[:band, pad:] - sums[band:, :pad]
        return mixed(real), mixed(imag)

    slot = 0

    def put(real, imag):
        nonlocal slot
        lhs_ref[:band, slot * pad : (slot + 1) * pad] = real
        lhs_ref[band:, slot * pad : (slot + 1) * pad] = imag
        slot += 1

    def put_both(real, imag):
        put(real, imag)
        fill = jnp.zeros((pad - band, pad), f32)
        real_t = jnp.transpose(jnp.concatenate([real, fill], axis=0))[:band]
        imag_t = jnp.transpose(jnp.concatenate([imag, fill], axis=0))[:band]
        put(real_t, -imag_t)

    if stacked:
        every = product(z_ref[...], zc_ref[...])
    depth = max(d for d in range(1, 17) if tiles % d == 0)
    for lag in range(SPAN):

        def part(step):
            left = z_ref[:, pl.ds(lane_tile(LAGS - lag + step * depth), depth * LANES)]
            right = zc_ref[:, pl.ds(lane_tile(step * depth), depth * LANES)]
            return product(left, right)

        if stacked:
            sums = every[2 * band * lag : 2 * band * (lag + 1)]
        else:
            sums = lax.fori_loop(
                0, tiles // depth, lambda step, total: total + part(step), jnp.zeros((2 * band, 2 * pad), f32)
            )
        pair = complex_gram(sums)
        if lag == 0:
            put(*pair)
        else:
            put_both(*pair)

    last = lines - 1
    spot = lax.broadcasted_iota(jnp.int32, (4 * band, LANES), 1) // readout
    top, bottom = spot == 0, spot == last // tiles

    here_top, here_bottom = [
        lax.broadcasted_iota(jnp.int32, (4 * pad, LANES), 1) // readout == group for group in (0, last // tiles)
    ]

    def outer_lines(low_tile, high_tile):
        parts = []
        for tile, where in ((low_tile, top), (high_tile, bottom)):
            start = tile * LANES if stacked else (LAGS + tile) * LANES
            value = [z_ref[at : at + 2 * band, start : start + LANES] for at in (0, 2 * held * band)]
            value = jnp.concatenate(value, axis=0).astype(f32)
            parts.append(jnp.where(where, value, 0.0).astype(jnp.bfloat16))
        right = zc_ref[:, high_tile * LANES : (high_tile + 1) * LANES].astype(f32)
        right = jnp.where(here_bottom, right, 0.0)
        right = jnp.where(here_top, zc_ref[:, low_tile * LANES : (low_tile + 1) * LANES].astype(f32), right)
        return parts[0], parts[1], right.astype(jnp.bfloat16)

    def stack(*lefts):
        rows_of = [left[at : at + 2 * band] for at in (0, 2 * band) for left in lefts]
        return jnp.concatenate(rows_of, axis=0)

    def cut(sums, index):
        return complex_gram(sums[2 * band * index : 2 * band * (index + 1)])

    top_0, bottom_0, right_0 = outer_lines(0, last % tiles)
    top_1, bottom_1, right_1 = outer_lines(1, (last - 1) % tiles)
    with_0 = product(stack(top_0, bottom_0, bottom_1), right_0)
    with_1 = product(stack(top_0, top_1, bottom_1), right_1)
    put(*cut(with_1, 2))
    put(*cut(with_0, 1))
    put(*cut(with_0, 0))
    put(*cut(with_1, 1))
    put_both(*cut(with_0, 2))
    put_both(*cut(with_1, 0))

    high, low = split(lhs_ref[...])
    lead = rhs_ref[:, : 2 * wide]
    total = lax.dot_general(high, lead, NN, preferred_element_type=f32)
    total += lax.dot_general(low, lead, NN, preferred_element_type=f32)
    total += lax.dot_general(high, rhs_ref[:, 2 * wide :], NN, preferred_element_type=f32)
    real = total[:band, :wide] + total[band:, wide:]
    imag = total[:band, wide:] - total[band:, :wide]

    factor = 1.0 / (SPAN**3 * scale)
    column = window % readout
    for part, values in enumerate((real, imag)):
        folded = jnp.zeros((cell, wide), f32)
        for e in range(SPAN):
            moved = values[e * cell : (e + 1) * cell]
            if e != HALF:
                moved = pltpu.roll(moved, (e - HALF) % wide, 1)
            near = column - e + HALF
            folded += jnp.where((near >= 0) & (near < readout), moved, 0.0)
        folded = folded * factor
        for line in range(rows):
            for f in range(frames):
                kept = measured_ref[part, :, line, f, :]
                at = (slice(f * coils, (f + 1) * coils), slice(line * readout, (line + 1) * readout))
                out_ref[part, :, line, f, :] = jnp.where(hit_ref[at] > 0, kept, folded[at])


def pack(lines_ref, estimate_ref, packed_ref, hit_ref):
    _, coils, rows, frames, readout = estimate_ref.shape
    shape = hit_ref.shape
    line = lax.axis_index("slab") * rows + lax.broadcasted_iota(jnp.int32, shape, 1) // readout
    frame = lax.broadcasted_iota(jnp.int32, shape, 0) // coils
    hit = jnp.zeros(shape, jnp.int32)
    for f in range(frames):
        for sample in range(lines_ref.shape[1]):
            hit = jnp.where((line == lines_ref[f, sample]) & (frame == f), 1, hit)
    hit_ref[...] = hit
    groups = LANES // readout
    for part in range(2):
        for f in range(frames):
            for line in range(rows):
                down, right = divmod((part * frames + f) * rows + line, groups)
                at = (0, slice(down * coils, (down + 1) * coils), slice(right * readout, (right + 1) * readout))
                packed_ref[at] = estimate_ref[part, :, line, f, :]
    packed = packed_ref[0]
    for copy in range(1, packed_ref.shape[0]):
        packed_ref[copy] = packed


def gather(copies):
    return lax.all_to_all(copies, "slab", 0, 0)


def stacks(tiles):
    return tiles <= 16


def local(estimate, measured, sampled_lines):
    _, coils, frames, rows, readout = estimate.shape
    slabs = lax.axis_size("slab")
    cell = coils * frames
    width = rows * readout
    band = SPAN * cell
    pad = up(band, LANES)
    wide = up(width, LANES)
    groups = LANES // readout
    tiles = up(slabs * rows, groups) // groups
    reach = up(LAGS, rows) // rows
    slots = 2 * SPAN - 1 + 8
    columns = (tiles if stacks(tiles) else LAGS + tiles) * LANES

    vmem = pl.BlockSpec(memory_space=pltpu.VMEM)
    packed, hit = pl.pallas_call(
        pack,
        out_shape=(
            jax.ShapeDtypeStruct((slabs, up(2 * frames * rows, groups) // groups * coils, LANES), jnp.float32),
            jax.ShapeDtypeStruct((cell, wide), jnp.int32),
        ),
        in_specs=[pl.BlockSpec(memory_space=pltpu.SMEM), vmem],
        out_specs=(vmem, vmem),
        compiler_params=pltpu.CompilerParams(vmem_limit_bytes=56 * 1024 * 1024),
        name="pack",
    )(sampled_lines, jnp.swapaxes(estimate, 2, 3))
    gathered = gather(packed)
    sizes = (slabs, coils, frames, rows, readout)
    result = pl.pallas_call(
        functools.partial(kernel, sizes),
        out_shape=jax.ShapeDtypeStruct((2, coils, rows, frames, readout), jnp.float32),
        in_specs=[vmem, vmem, vmem],
        out_specs=vmem,
        scratch_shapes=[
            pltpu.VMEM((2 * cell, (LAGS + tiles) * LANES), jnp.float32),
            pltpu.VMEM((4 * band * (SPAN if stacks(tiles) else 1), columns), jnp.bfloat16),
            pltpu.VMEM((4 * pad, tiles * LANES), jnp.bfloat16),
            pltpu.VMEM((2 * cell, LANES), jnp.float32),
            pltpu.VMEM((2 * cell, up((2 * reach + 1) * width + LANES, LANES)), jnp.float32),
            pltpu.VMEM((2 * band, slots * pad), jnp.float32),
            pltpu.VMEM((slots * pad, 4 * wide), jnp.bfloat16),
        ],
        compiler_params=pltpu.CompilerParams(vmem_limit_bytes=40 * 1024 * 1024),
        name="filter_step",
    )(hit, gathered, jnp.swapaxes(measured, 2, 3))
    return jnp.swapaxes(result, 2, 3)


def solution(mesh):
    placed = (
        P(None, None, "grp", "slab", None),
        P(None, None, "grp", "slab", None),
        P("grp", None),
    )
    return jax.shard_map(
        local,
        mesh=mesh,
        in_specs=placed,
        out_specs=P(None, None, "grp", "slab", None),
        check_vma=False,
    )
```

```python
import functools

import jax
import jax.numpy as jnp
from jax import lax
from jax.experimental import pallas as pl
from jax.experimental.pallas import tpu as pltpu
from jax.sharding import PartitionSpec as P

SPAN = 5
HALF = SPAN // 2
LAGS = SPAN - 1
LANES = 128
NT = (((1,), (1,)), ((), ()))
NN = (((1,), (0,)), ((), ()))


def up(size, unit):
    return -(-size // unit) * unit


def split(value):
    high = value.astype(jnp.bfloat16)
    return high, (value - high.astype(jnp.float32)).astype(jnp.bfloat16)


def repeat(count, body):
    if count <= 16:
        for step in range(count):
            body(step)
    else:
        lax.fori_loop(0, count, lambda step, carry: (body(step), carry)[1], 0)


def lane_tile(tile):
    start = tile * LANES
    return start if isinstance(start, int) else pl.multiple_of(start, LANES)


def kernel(sizes, hit_ref, gathered_ref, measured_ref, result_ref, x_ref, z_ref, zc_ref, acc_ref, xw_ref, lhs_ref, rhs_ref, out_ref, sems):
    slabs, coils, frames, rows, readout = sizes
    me = lax.axis_index("slab")
    cell = coils * frames
    band = SPAN * cell
    pad = up(band, LANES)
    width = rows * readout
    groups = LANES // readout
    lines = slabs * rows
    tiles = up(lines, groups) // groups
    f32 = jnp.float32

    planes = 2 * frames

    def unpacked(block, plane, line):
        down, right = divmod(plane * rows + line, groups)
        return gathered_ref[block, down * coils : (down + 1) * coils, right * readout : (right + 1) * readout]

    if tiles * groups != lines:
        x_ref[...] = jnp.zeros_like(x_ref)
    for line in range(lines):
        block, inner = divmod(line, rows)
        group, tile = divmod(line, tiles)
        start = (LAGS + tile) * LANES + group * readout
        for plane in range(planes):
            x_ref[plane * coils : (plane + 1) * coils, start : start + readout] = unpacked(block, plane, inner)
    lane = lax.broadcasted_iota(jnp.int32, (2 * cell, LANES), 1)
    for back in range(1, LAGS + 1):
        source = (LAGS + tiles - back) * LANES
        wrapped = pltpu.roll(x_ref[:, source : source + LANES], readout, 1)
        target = (LAGS - back) * LANES
        x_ref[:, target : target + LANES] = jnp.where(lane >= readout, wrapped, 0.0)

    column = lane % readout
    inside = [(column + e - HALF >= 0) & (column + e - HALF < readout) for e in range(SPAN)]

    stacked = stacks(tiles)
    held = SPAN if stacked else 1

    def patches(tile):
        source = pl.ds(lane_tile(tile), LANES)
        if stacked:
            targets = [(lag, tile - LAGS + lag) for lag in range(SPAN) if 0 <= tile - LAGS + lag < tiles]
        else:
            targets = [(0, tile)]
        cells = x_ref[:, source]
        for e in range(SPAN):
            moved = cells if e == HALF else pltpu.roll(cells, (HALF - e) % LANES, 1)
            high, low = split(jnp.where(inside[e], moved, 0.0))
            for lag, target in targets:
                at = pl.ds(lane_tile(target), LANES)
                for part in range(2):
                    first = (2 * lag + part) * band + e * cell
                    z_ref[first : first + cell, at] = high[part * cell : (part + 1) * cell]
                    first += 2 * held * band
                    z_ref[first : first + cell, at] = low[part * cell : (part + 1) * cell]
            if stacked and tile >= LAGS:
                at = pl.ds(lane_tile(tile - LAGS), LANES)
                for part in range(2):
                    first = part * pad + e * cell
                    zc_ref[first : first + cell, at] = high[part * cell : (part + 1) * cell]
                    first += 2 * pad
                    zc_ref[first : first + cell, at] = low[part * cell : (part + 1) * cell]

    if stacked:
        for tile in range(LAGS + tiles):
            patches(tile)
    else:
        repeat(LAGS + tiles, patches)

    def centre(tile):
        source = pl.ds(lane_tile(tile + LAGS), LANES)
        at = pl.ds(lane_tile(tile), LANES)
        for piece in range(4):
            first = piece * pad
            if not stacked:
                zc_ref[first : first + band, at] = z_ref[piece * band : (piece + 1) * band, source]
            zc_ref[first + band : first + pad, at] = jnp.zeros((pad - band, LANES), jnp.bfloat16)

    repeat(tiles, centre)

    line_base = lane // readout * tiles
    acc_ref[...] = jnp.zeros_like(acc_ref)

    def energy(tile):
        cells = x_ref[:, pl.ds(lane_tile(tile + LAGS), LANES)]
        line = line_base + tile
        covers = jnp.minimum(line + HALF, lines - 1) - jnp.maximum(line - HALF, 0) + 1
        acc_ref[...] += cells * cells * covers.astype(f32)

    repeat(tiles, energy)
    row = lax.broadcasted_iota(jnp.int32, (2 * cell, LANES), 0)
    frame = row // coils % frames
    covers_t = jnp.minimum(frame + HALF, frames - 1) - jnp.maximum(frame - HALF, 0) + 1
    covers_x = jnp.minimum(column + HALF, readout - 1) - jnp.maximum(column - HALF, 0) + 1
    weighted = acc_ref[...] * (covers_t * covers_x).astype(f32)
    trace = jnp.sum(jnp.sum(weighted, axis=1, keepdims=True), axis=0, keepdims=True)
    scale = trace / (SPAN**3 * coils) + 1e-06

    def product(left, right):
        half = left.shape[0] // 2
        both = lax.dot_general(left, right[: 2 * pad], NT, preferred_element_type=f32)
        cross = lax.dot_general(left[:half], right[2 * pad :], NT, preferred_element_type=f32)
        return both[:half] + both[half:] + cross

    mrow = lax.broadcasted_iota(jnp.int32, (band, pad), 0) // coils % frames
    mcol = lax.broadcasted_iota(jnp.int32, (band, pad), 1) // coils % frames
    mixes = []
    for shift in range(-frames + 1, frames):
        mask = jnp.zeros((band, pad), f32)
        for i in range(frames):
            for j in range(frames):
                if 0 <= i + shift < frames and 0 <= j + shift < frames:
                    count = sum(
                        abs(i - t) <= HALF and abs(j - t) <= HALF and 0 <= t + shift < frames for t in range(frames)
                    )
                    mask = jnp.where((mrow == i) & (mcol == j), float(count), mask)
        mixes.append((shift, mask))

    def mixed(gram):
        total = None
        for shift, mask in mixes:
            moved = gram
            if shift:
                moved = pltpu.roll(pltpu.roll(gram, -shift * coils % pad, 1), -shift * coils % band, 0)
            total = moved * mask if total is None else total + moved * mask
        return total

    def complex_gram(sums):
        real = sums[:band, :pad] + sums[band:, pad:]
        imag = sums[:band, pad:] - sums[band:, :pad]
        return mixed(real), mixed(imag)

    slot = 0
    order = []

    def put(real, imag, lag, weight):
        nonlocal slot
        lhs_ref[:band, slot * pad : (slot + 1) * pad] = real
        lhs_ref[band:, slot * pad : (slot + 1) * pad] = imag
        order.append((lag, weight))
        slot += 1

    def put_both(pair, lag, weight, back_weight):
        real, imag = pair
        put(real, imag, lag, weight)
        fill = jnp.zeros((pad - band, pad), f32)
        real_t = jnp.transpose(jnp.concatenate([real, fill], axis=0))[:band]
        imag_t = jnp.transpose(jnp.concatenate([imag, fill], axis=0))[:band]
        put(real_t, -imag_t, -lag, back_weight)

    window = lax.broadcasted_iota(jnp.int32, (cell, up(width, LANES)), 1)
    my_line = me * rows + window // readout
    valid = [((my_line - b + HALF >= 0) & (my_line - b + HALF < lines)).astype(f32) for b in range(SPAN)]

    def lag_weight(lag):
        total = None
        for b in range(SPAN):
            if 0 <= b + lag < SPAN:
                total = valid[b] if total is None else total + valid[b]
        return total

    if stacked:
        every = product(z_ref[...], zc_ref[...])
    depth = max(d for d in range(1, 17) if tiles % d == 0)
    for lag in range(SPAN):

        def part(step):
            left = z_ref[:, pl.ds(lane_tile(LAGS - lag + step * depth), depth * LANES)]
            right = zc_ref[:, pl.ds(lane_tile(step * depth), depth * LANES)]
            return product(left, right)

        if stacked:
            sums = every[2 * band * lag : 2 * band * (lag + 1)]
        else:
            sums = lax.fori_loop(
                0, tiles // depth, lambda step, total: total + part(step), jnp.zeros((2 * band, 2 * pad), f32)
            )
        pair = complex_gram(sums)
        if lag == 0:
            put(*pair, 0, lag_weight(0))
        else:
            put_both(pair, lag, lag_weight(lag), lag_weight(-lag))

    def edge(first, second):
        group, tile = divmod(first, tiles)
        other = second % tiles
        start = tile * LANES if stacked else (LAGS + tile) * LANES
        here = lax.broadcasted_iota(jnp.int32, (2 * band, LANES), 1) // readout == group
        halves = []
        for base in (0, 2 * held * band):
            value = z_ref[base : base + 2 * band, start : start + LANES].astype(f32)
            halves.append(jnp.where(here, value, 0.0).astype(jnp.bfloat16))
        left = jnp.concatenate(halves, axis=0)
        return complex_gram(product(left, zc_ref[:, other * LANES : (other + 1) * LANES]))

    last = lines - 1
    put(*edge(last - 1, last - 1), 0, -valid[0])
    put(*edge(last, last), 0, -(valid[0] + valid[1]))
    put(*edge(0, 0), 0, -(valid[3] + valid[4]))
    put(*edge(1, 1), 0, -valid[4])
    put_both(edge(last - 1, last), 1, -valid[0], -valid[1])
    put_both(edge(0, 1), 1, -valid[3], -valid[4])

    reach = up(LAGS, rows) // rows
    for j in range(-reach, reach + 1):
        block = me + j
        exists = (block >= 0) & (block < slabs)
        block = jnp.clip(block, 0, slabs - 1)
        for line in range(rows):
            start = (j + reach) * width + line * readout
            for plane in range(planes):
                held = jnp.where(exists, unpacked(block, plane, line), 0.0)
                xw_ref[plane * coils : (plane + 1) * coils, start : start + readout] = held
    extent = xw_ref.shape[1]
    spread = lax.broadcasted_iota(jnp.int32, (2 * cell, extent), 1) % readout
    around = xw_ref[...]
    wide = up(width, LANES)
    for e in range(SPAN):
        moved = around if e == HALF else pltpu.roll(around, (HALF - e) % extent, 1)
        near = spread + e - HALF
        moved = jnp.where((near >= 0) & (near < readout), moved, 0.0)
        for lag in range(-LAGS, LAGS + 1):
            start = (reach * rows + lag) * readout
            piece = moved[:, start : start + wide]
            for index, (at, weight) in enumerate(order):
                if at == lag:
                    first = index * pad + e * cell
                    for part in range(2):
                        high, low = split(piece[part * cell : (part + 1) * cell] * weight)
                        rhs_ref[first : first + cell, part * wide : (part + 1) * wide] = high
                        rhs_ref[first : first + cell, (2 + part) * wide : (3 + part) * wide] = low
    for index in range(len(order)):
        first = index * pad
        rhs_ref[first + band : first + pad, :] = jnp.zeros((pad - band, 4 * wide), jnp.bfloat16)

    high, low = split(lhs_ref[...])
    lead = rhs_ref[:, : 2 * wide]
    total = lax.dot_general(high, lead, NN, preferred_element_type=f32)
    total += lax.dot_general(low, lead, NN, preferred_element_type=f32)
    total += lax.dot_general(high, rhs_ref[:, 2 * wide :], NN, preferred_element_type=f32)
    real = total[:band, :wide] + total[band:, wide:]
    imag = total[:band, wide:] - total[band:, :wide]

    factor = 1.0 / (SPAN**3 * scale)
    column = window % readout
    leaving = []
    for part, values in enumerate((real, imag)):
        folded = jnp.zeros((cell, wide), f32)
        for e in range(SPAN):
            moved = values[e * cell : (e + 1) * cell]
            if e != HALF:
                moved = pltpu.roll(moved, (e - HALF) % wide, 1)
            near = column - e + HALF
            folded += jnp.where((near >= 0) & (near < readout), moved, 0.0)
        folded = folded * factor
        for line in range(rows):
            for f in range(frames):
                kept = measured_ref[part, :, line, f, :]
                at = (slice(f * coils, (f + 1) * coils), slice(line * readout, (line + 1) * readout))
                out_ref[part, :, line, f, :] = jnp.where(hit_ref[at] > 0, kept, folded[at])
        leaving.append(pltpu.make_async_copy(out_ref.at[part], result_ref.at[part], sems.at[part]))
        leaving[part].start()
    for copy in leaving:
        copy.wait()


def pack(table_ref, source_ref, blocks_ref, mask_ref, lines_ref, estimate_ref, packed_ref, hit_ref, sems):
    coming = pltpu.make_async_copy(source_ref, estimate_ref, sems.at[0])
    coming.start()
    table = pltpu.make_async_copy(table_ref, lines_ref, sems.at[1])
    table.start()
    _, coils, rows, frames, readout = estimate_ref.shape
    groups = LANES // readout
    coming.wait()
    for part in range(2):
        for f in range(frames):
            for line in range(rows):
                down, right = divmod((part * frames + f) * rows + line, groups)
                at = (0, slice(down * coils, (down + 1) * coils), slice(right * readout, (right + 1) * readout))
                packed_ref[at] = estimate_ref[part, :, line, f, :]
    packed = packed_ref[0]
    for copy in range(1, packed_ref.shape[0]):
        packed_ref[copy] = packed
    leaving = pltpu.make_async_copy(packed_ref, blocks_ref, sems.at[2])
    leaving.start()
    table.wait()
    shape = hit_ref.shape
    line = lax.axis_index("slab") * rows + lax.broadcasted_iota(jnp.int32, shape, 1) // readout
    frame = lax.broadcasted_iota(jnp.int32, shape, 0) // coils
    hit = jnp.zeros(shape, jnp.int32)
    for f in range(frames):
        for sample in range(lines_ref.shape[1]):
            hit = jnp.where((line == lines_ref[f, sample]) & (frame == f), 1, hit)
    hit_ref[...] = hit
    marking = pltpu.make_async_copy(hit_ref, mask_ref, sems.at[3])
    marking.start()
    leaving.wait()
    marking.wait()


def gather(copies):
    return lax.all_to_all(copies, "slab", 0, 0)


def stacks(tiles):
    return tiles <= 16


def local(estimate, measured, sampled_lines):
    _, coils, frames, rows, readout = estimate.shape
    slabs = lax.axis_size("slab")
    cell = coils * frames
    width = rows * readout
    band = SPAN * cell
    pad = up(band, LANES)
    wide = up(width, LANES)
    groups = LANES // readout
    tiles = up(slabs * rows, groups) // groups
    reach = up(LAGS, rows) // rows
    slots = 2 * SPAN - 1 + 8
    columns = (tiles if stacks(tiles) else LAGS + tiles) * LANES

    vmem = pl.BlockSpec(memory_space=pltpu.VMEM)
    blocks = (slabs, up(2 * frames * rows, groups) // groups * coils, LANES)
    hbm = pl.BlockSpec(memory_space=pl.ANY)
    packed, hit = pl.pallas_call(
        pack,
        out_shape=(jax.ShapeDtypeStruct(blocks, jnp.float32), jax.ShapeDtypeStruct((cell, wide), jnp.int32)),
        in_specs=[hbm, hbm],
        out_specs=(hbm, hbm),
        scratch_shapes=[
            pltpu.SMEM(sampled_lines.shape, jnp.int32),
            pltpu.VMEM((2, coils, rows, frames, readout), jnp.float32),
            pltpu.VMEM(blocks, jnp.float32),
            pltpu.VMEM((cell, wide), jnp.int32),
            pltpu.SemaphoreType.DMA((4,)),
        ],
        compiler_params=pltpu.CompilerParams(vmem_limit_bytes=56 * 1024 * 1024),
        name="pack",
    )(sampled_lines, jnp.swapaxes(estimate, 2, 3))
    gathered = gather(packed)
    sizes = (slabs, coils, frames, rows, readout)
    result = pl.pallas_call(
        functools.partial(kernel, sizes),
        out_shape=jax.ShapeDtypeStruct((2, coils, rows, frames, readout), jnp.float32),
        in_specs=[vmem, vmem, vmem],
        out_specs=hbm,
        scratch_shapes=[
            pltpu.VMEM((2 * cell, (LAGS + tiles) * LANES), jnp.float32),
            pltpu.VMEM((4 * band * (SPAN if stacks(tiles) else 1), columns), jnp.bfloat16),
            pltpu.VMEM((4 * pad, tiles * LANES), jnp.bfloat16),
            pltpu.VMEM((2 * cell, LANES), jnp.float32),
            pltpu.VMEM((2 * cell, up((2 * reach + 1) * width + LANES, LANES)), jnp.float32),
            pltpu.VMEM((2 * band, slots * pad), jnp.float32),
            pltpu.VMEM((slots * pad, 4 * wide), jnp.bfloat16),
            pltpu.VMEM((2, coils, rows, frames, readout), jnp.float32),
            pltpu.SemaphoreType.DMA((2,)),
        ],
        compiler_params=pltpu.CompilerParams(vmem_limit_bytes=40 * 1024 * 1024),
        name="filter_step",
    )(hit, gathered, jnp.swapaxes(measured, 2, 3))
    return jnp.swapaxes(result, 2, 3)


def solution(mesh):
    placed = (
        P(None, None, "grp", "slab", None),
        P(None, None, "grp", "slab", None),
        P("grp", None),
    )
    return jax.shard_map(
        local,
        mesh=mesh,
        in_specs=placed,
        out_specs=P(None, None, "grp", "slab", None),
        check_vma=False,
    )
```

```python
import functools

import jax
import jax.numpy as jnp
from jax import lax
from jax.experimental import pallas as pl
from jax.experimental.pallas import tpu as pltpu
from jax.sharding import PartitionSpec as P

SPAN = 5
HALF = SPAN // 2
LAGS = SPAN - 1
LANES = 128
NT = (((1,), (1,)), ((), ()))
NN = (((1,), (0,)), ((), ()))


def up(size, unit):
    return -(-size // unit) * unit


def split(value):
    high = value.astype(jnp.bfloat16)
    return high, (value - high.astype(jnp.float32)).astype(jnp.bfloat16)


def repeat(count, body):
    if count <= 16:
        for step in range(count):
            body(step)
    else:
        lax.fori_loop(0, count, lambda step, carry: (body(step), carry)[1], 0)


def lane_tile(tile):
    start = tile * LANES
    return start if isinstance(start, int) else pl.multiple_of(start, LANES)


def kernel(sizes, hit_ref, gathered_ref, measured_ref, out_ref, x_ref, z_ref, zc_ref, acc_ref, xw_ref, lhs_ref, rhs_ref):
    slabs, coils, frames, rows, readout = sizes
    me = lax.axis_index("slab")
    cell = coils * frames
    band = SPAN * cell
    pad = up(band, LANES)
    width = rows * readout
    groups = LANES // readout
    lines = slabs * rows
    tiles = up(lines, groups) // groups
    f32 = jnp.float32

    planes = 2 * frames

    def unpacked(block, plane, line):
        down, right = divmod(plane * rows + line, groups)
        return gathered_ref[place(block, slabs), down * coils : (down + 1) * coils, right * readout : (right + 1) * readout]

    if tiles * groups != lines:
        x_ref[...] = jnp.zeros_like(x_ref)
    for line in range(lines):
        block, inner = divmod(line, rows)
        group, tile = divmod(line, tiles)
        start = (LAGS + tile) * LANES + group * readout
        for plane in range(planes):
            x_ref[plane * coils : (plane + 1) * coils, start : start + readout] = unpacked(block, plane, inner)
    lane = lax.broadcasted_iota(jnp.int32, (2 * cell, LANES), 1)
    for back in range(1, LAGS + 1):
        source = (LAGS + tiles - back) * LANES
        wrapped = pltpu.roll(x_ref[:, source : source + LANES], readout, 1)
        target = (LAGS - back) * LANES
        x_ref[:, target : target + LANES] = jnp.where(lane >= readout, wrapped, 0.0)

    column = lane % readout
    inside = [(column + e - HALF >= 0) & (column + e - HALF < readout) for e in range(SPAN)]

    stacked = stacks(tiles)
    held = SPAN if stacked else 1

    def patches(tile):
        source = pl.ds(lane_tile(tile), LANES)
        if stacked:
            targets = [(lag, tile - LAGS + lag) for lag in range(SPAN) if 0 <= tile - LAGS + lag < tiles]
        else:
            targets = [(0, tile)]
        cells = x_ref[:, source]
        for e in range(SPAN):
            moved = cells if e == HALF else pltpu.roll(cells, (HALF - e) % LANES, 1)
            high, low = split(jnp.where(inside[e], moved, 0.0))
            for lag, target in targets:
                at = pl.ds(lane_tile(target), LANES)
                for part in range(2):
                    first = (2 * lag + part) * band + e * cell
                    z_ref[first : first + cell, at] = high[part * cell : (part + 1) * cell]
                    first += 2 * held * band
                    z_ref[first : first + cell, at] = low[part * cell : (part + 1) * cell]
            if stacked and tile >= LAGS:
                at = pl.ds(lane_tile(tile - LAGS), LANES)
                for part in range(2):
                    first = part * pad + e * cell
                    zc_ref[first : first + cell, at] = high[part * cell : (part + 1) * cell]
                    first += 2 * pad
                    zc_ref[first : first + cell, at] = low[part * cell : (part + 1) * cell]

    if stacked:
        for tile in range(LAGS + tiles):
            patches(tile)
    else:
        repeat(LAGS + tiles, patches)

    def centre(tile):
        source = pl.ds(lane_tile(tile + LAGS), LANES)
        at = pl.ds(lane_tile(tile), LANES)
        for piece in range(4):
            first = piece * pad
            if not stacked:
                zc_ref[first : first + band, at] = z_ref[piece * band : (piece + 1) * band, source]
            zc_ref[first + band : first + pad, at] = jnp.zeros((pad - band, LANES), jnp.bfloat16)

    repeat(tiles, centre)

    line_base = lane // readout * tiles
    acc_ref[...] = jnp.zeros_like(acc_ref)

    def energy(tile):
        cells = x_ref[:, pl.ds(lane_tile(tile + LAGS), LANES)]
        line = line_base + tile
        covers = jnp.minimum(line + HALF, lines - 1) - jnp.maximum(line - HALF, 0) + 1
        acc_ref[...] += cells * cells * covers.astype(f32)

    repeat(tiles, energy)
    row = lax.broadcasted_iota(jnp.int32, (2 * cell, LANES), 0)
    frame = row // coils % frames
    covers_t = jnp.minimum(frame + HALF, frames - 1) - jnp.maximum(frame - HALF, 0) + 1
    covers_x = jnp.minimum(column + HALF, readout - 1) - jnp.maximum(column - HALF, 0) + 1
    weighted = acc_ref[...] * (covers_t * covers_x).astype(f32)
    trace = jnp.sum(jnp.sum(weighted, axis=1, keepdims=True), axis=0, keepdims=True)
    scale = trace / (SPAN**3 * coils) + 1e-06

    def product(left, right):
        half = left.shape[0] // 2
        both = lax.dot_general(left, right[: 2 * pad], NT, preferred_element_type=f32)
        cross = lax.dot_general(left[:half], right[2 * pad :], NT, preferred_element_type=f32)
        return both[:half] + both[half:] + cross

    mrow = lax.broadcasted_iota(jnp.int32, (band, pad), 0) // coils % frames
    mcol = lax.broadcasted_iota(jnp.int32, (band, pad), 1) // coils % frames
    mixes = []
    for shift in range(-frames + 1, frames):
        mask = jnp.zeros((band, pad), f32)
        for i in range(frames):
            for j in range(frames):
                if 0 <= i + shift < frames and 0 <= j + shift < frames:
                    count = sum(
                        abs(i - t) <= HALF and abs(j - t) <= HALF and 0 <= t + shift < frames for t in range(frames)
                    )
                    mask = jnp.where((mrow == i) & (mcol == j), float(count), mask)
        mixes.append((shift, mask))

    def mixed(gram):
        total = None
        for shift, mask in mixes:
            moved = gram
            if shift:
                moved = pltpu.roll(pltpu.roll(gram, -shift * coils % pad, 1), -shift * coils % band, 0)
            total = moved * mask if total is None else total + moved * mask
        return total

    def complex_gram(sums):
        real = sums[:band, :pad] + sums[band:, pad:]
        imag = sums[:band, pad:] - sums[band:, :pad]
        return mixed(real), mixed(imag)

    slot = 0
    order = []

    def put(real, imag, lag, weight):
        nonlocal slot
        lhs_ref[:band, slot * pad : (slot + 1) * pad] = real
        lhs_ref[band:, slot * pad : (slot + 1) * pad] = imag
        order.append((lag, weight))
        slot += 1

    def put_both(pair, lag, weight, back_weight):
        real, imag = pair
        put(real, imag, lag, weight)
        fill = jnp.zeros((pad - band, pad), f32)
        real_t = jnp.transpose(jnp.concatenate([real, fill], axis=0))[:band]
        imag_t = jnp.transpose(jnp.concatenate([imag, fill], axis=0))[:band]
        put(real_t, -imag_t, -lag, back_weight)

    window = lax.broadcasted_iota(jnp.int32, (cell, up(width, LANES)), 1)
    my_line = me * rows + window // readout
    valid = [((my_line - b + HALF >= 0) & (my_line - b + HALF < lines)).astype(f32) for b in range(SPAN)]

    def lag_weight(lag):
        total = None
        for b in range(SPAN):
            if 0 <= b + lag < SPAN:
                total = valid[b] if total is None else total + valid[b]
        return total

    if stacked:
        every = product(z_ref[...], zc_ref[...])
    depth = max(d for d in range(1, 17) if tiles % d == 0)
    for lag in range(SPAN):

        def part(step):
            left = z_ref[:, pl.ds(lane_tile(LAGS - lag + step * depth), depth * LANES)]
            right = zc_ref[:, pl.ds(lane_tile(step * depth), depth * LANES)]
            return product(left, right)

        if stacked:
            sums = every[2 * band * lag : 2 * band * (lag + 1)]
        else:
            sums = lax.fori_loop(
                0, tiles // depth, lambda step, total: total + part(step), jnp.zeros((2 * band, 2 * pad), f32)
            )
        pair = complex_gram(sums)
        if lag == 0:
            put(*pair, 0, lag_weight(0))
        else:
            put_both(pair, lag, lag_weight(lag), lag_weight(-lag))

    def edge(first, second):
        group, tile = divmod(first, tiles)
        other = second % tiles
        start = tile * LANES if stacked else (LAGS + tile) * LANES
        here = lax.broadcasted_iota(jnp.int32, (2 * band, LANES), 1) // readout == group
        halves = []
        for base in (0, 2 * held * band):
            value = z_ref[base : base + 2 * band, start : start + LANES].astype(f32)
            halves.append(jnp.where(here, value, 0.0).astype(jnp.bfloat16))
        left = jnp.concatenate(halves, axis=0)
        return complex_gram(product(left, zc_ref[:, other * LANES : (other + 1) * LANES]))

    last = lines - 1
    put(*edge(last - 1, last - 1), 0, -valid[0])
    put(*edge(last, last), 0, -(valid[0] + valid[1]))
    put(*edge(0, 0), 0, -(valid[3] + valid[4]))
    put(*edge(1, 1), 0, -valid[4])
    put_both(edge(last - 1, last), 1, -valid[0], -valid[1])
    put_both(edge(0, 1), 1, -valid[3], -valid[4])

    reach = up(LAGS, rows) // rows
    for j in range(-reach, reach + 1):
        block = me + j
        exists = (block >= 0) & (block < slabs)
        block = jnp.clip(block, 0, slabs - 1)
        for line in range(rows):
            start = (j + reach) * width + line * readout
            for plane in range(planes):
                held = jnp.where(exists, unpacked(block, plane, line), 0.0)
                xw_ref[plane * coils : (plane + 1) * coils, start : start + readout] = held
    extent = xw_ref.shape[1]
    spread = lax.broadcasted_iota(jnp.int32, (2 * cell, extent), 1) % readout
    around = xw_ref[...]
    wide = up(width, LANES)
    for e in range(SPAN):
        moved = around if e == HALF else pltpu.roll(around, (HALF - e) % extent, 1)
        near = spread + e - HALF
        moved = jnp.where((near >= 0) & (near < readout), moved, 0.0)
        for lag in range(-LAGS, LAGS + 1):
            start = (reach * rows + lag) * readout
            piece = moved[:, start : start + wide]
            for index, (at, weight) in enumerate(order):
                if at == lag:
                    first = index * pad + e * cell
                    for part in range(2):
                        high, low = split(piece[part * cell : (part + 1) * cell] * weight)
                        rhs_ref[first : first + cell, part * wide : (part + 1) * wide] = high
                        rhs_ref[first : first + cell, (2 + part) * wide : (3 + part) * wide] = low
    for index in range(len(order)):
        first = index * pad
        rhs_ref[first + band : first + pad, :] = jnp.zeros((pad - band, 4 * wide), jnp.bfloat16)

    high, low = split(lhs_ref[...])
    lead = rhs_ref[:, : 2 * wide]
    total = lax.dot_general(high, lead, NN, preferred_element_type=f32)
    total += lax.dot_general(low, lead, NN, preferred_element_type=f32)
    total += lax.dot_general(high, rhs_ref[:, 2 * wide :], NN, preferred_element_type=f32)
    real = total[:band, :wide] + total[band:, wide:]
    imag = total[:band, wide:] - total[band:, :wide]

    factor = 1.0 / (SPAN**3 * scale)
    column = window % readout
    for part, values in enumerate((real, imag)):
        folded = jnp.zeros((cell, wide), f32)
        for e in range(SPAN):
            moved = values[e * cell : (e + 1) * cell]
            if e != HALF:
                moved = pltpu.roll(moved, (e - HALF) % wide, 1)
            near = column - e + HALF
            folded += jnp.where((near >= 0) & (near < readout), moved, 0.0)
        folded = folded * factor
        for line in range(rows):
            for f in range(frames):
                kept = measured_ref[part, :, line, f, :]
                at = (slice(f * coils, (f + 1) * coils), slice(line * readout, (line + 1) * readout))
                out_ref[part, :, line, f, :] = jnp.where(hit_ref[at] > 0, kept, folded[at])


def pack(lines_ref, estimate_ref, packed_ref, hit_ref):
    _, coils, rows, frames, readout = estimate_ref.shape
    shape = hit_ref.shape
    line = lax.axis_index("slab") * rows + lax.broadcasted_iota(jnp.int32, shape, 1) // readout
    frame = lax.broadcasted_iota(jnp.int32, shape, 0) // coils
    hit = jnp.zeros(shape, jnp.int32)
    for f in range(frames):
        for sample in range(lines_ref.shape[1]):
            hit = jnp.where((line == lines_ref[f, sample]) & (frame == f), 1, hit)
    hit_ref[...] = hit
    groups = LANES // readout
    for part in range(2):
        for f in range(frames):
            for line in range(rows):
                down, right = divmod((part * frames + f) * rows + line, groups)
                at = (0, slice(down * coils, (down + 1) * coils), slice(right * readout, (right + 1) * readout))
                packed_ref[at] = estimate_ref[part, :, line, f, :]
    packed = packed_ref[0]
    for copy in range(1, packed_ref.shape[0]):
        packed_ref[copy] = packed


def steps(slabs):
    return [(slabs // 4, 4), (2, 2), (2, 1)] if slabs % 4 == 0 else [(slabs, 1)]


def place(block, slabs):
    spot, weight = 0, 1
    for size, stride in steps(slabs):
        spot += block // stride % size * weight
        weight *= size
    return spot


def gather(held):
    slabs = lax.axis_size("slab")
    for size, stride in steps(slabs):
        firsts = [i for i in range(slabs) if i // stride % size == 0]
        groups = [[i + j * stride for j in range(size)] for i in firsts]
        held = lax.all_gather(held, "slab", axis_index_groups=groups, tiled=True)
    return held


def stacks(tiles):
    return tiles <= 16


def local(estimate, measured, sampled_lines):
    _, coils, frames, rows, readout = estimate.shape
    slabs = lax.axis_size("slab")
    cell = coils * frames
    width = rows * readout
    band = SPAN * cell
    pad = up(band, LANES)
    wide = up(width, LANES)
    groups = LANES // readout
    tiles = up(slabs * rows, groups) // groups
    reach = up(LAGS, rows) // rows
    slots = 2 * SPAN - 1 + 8
    columns = (tiles if stacks(tiles) else LAGS + tiles) * LANES

    vmem = pl.BlockSpec(memory_space=pltpu.VMEM)
    packed, hit = pl.pallas_call(
        pack,
        out_shape=(
            jax.ShapeDtypeStruct((1, up(2 * frames * rows, groups) // groups * coils, LANES), jnp.float32),
            jax.ShapeDtypeStruct((cell, wide), jnp.int32),
        ),
        in_specs=[pl.BlockSpec(memory_space=pltpu.SMEM), vmem],
        out_specs=(vmem, vmem),
        compiler_params=pltpu.CompilerParams(vmem_limit_bytes=56 * 1024 * 1024),
        name="pack",
    )(sampled_lines, jnp.swapaxes(estimate, 2, 3))
    gathered = gather(packed)
    sizes = (slabs, coils, frames, rows, readout)
    result = pl.pallas_call(
        functools.partial(kernel, sizes),
        out_shape=jax.ShapeDtypeStruct((2, coils, rows, frames, readout), jnp.float32),
        in_specs=[vmem, vmem, vmem],
        out_specs=vmem,
        scratch_shapes=[
            pltpu.VMEM((2 * cell, (LAGS + tiles) * LANES), jnp.float32),
            pltpu.VMEM((4 * band * (SPAN if stacks(tiles) else 1), columns), jnp.bfloat16),
            pltpu.VMEM((4 * pad, tiles * LANES), jnp.bfloat16),
            pltpu.VMEM((2 * cell, LANES), jnp.float32),
            pltpu.VMEM((2 * cell, up((2 * reach + 1) * width + LANES, LANES)), jnp.float32),
            pltpu.VMEM((2 * band, slots * pad), jnp.float32),
            pltpu.VMEM((slots * pad, 4 * wide), jnp.bfloat16),
        ],
        compiler_params=pltpu.CompilerParams(vmem_limit_bytes=40 * 1024 * 1024),
        name="filter_step",
    )(hit, gathered, jnp.swapaxes(measured, 2, 3))
    return jnp.swapaxes(result, 2, 3)


def solution(mesh):
    placed = (
        P(None, None, "grp", "slab", None),
        P(None, None, "grp", "slab", None),
        P("grp", None),
    )
    return jax.shard_map(
        local,
        mesh=mesh,
        in_specs=placed,
        out_specs=P(None, None, "grp", "slab", None),
        check_vma=False,
    )
```

```python
import functools

import jax
import jax.numpy as jnp
from jax import lax
from jax.experimental import pallas as pl
from jax.experimental.pallas import tpu as pltpu
from jax.sharding import PartitionSpec as P

SPAN = 5
HALF = SPAN // 2
LAGS = SPAN - 1
LANES = 128
NT = (((1,), (1,)), ((), ()))
NN = (((1,), (0,)), ((), ()))


def up(size, unit):
    return -(-size // unit) * unit


def split(value):
    high = value.astype(jnp.bfloat16)
    return high, (value - high.astype(jnp.float32)).astype(jnp.bfloat16)


def repeat(count, body):
    if count <= 16:
        for step in range(count):
            body(step)
    else:
        lax.fori_loop(0, count, lambda step, carry: (body(step), carry)[1], 0)


def lane_tile(tile):
    start = tile * LANES
    return start if isinstance(start, int) else pl.multiple_of(start, LANES)


def kernel(sizes, hit_ref, gathered_ref, measured_ref, out_ref, x_ref, z_ref, zc_ref, acc_ref, xw_ref, lhs_ref, rhs_ref):
    slabs, coils, frames, rows, readout = sizes
    me = lax.axis_index("slab")
    cell = coils * frames
    band = SPAN * cell
    pad = up(band, LANES)
    width = rows * readout
    groups = LANES // readout
    lines = slabs * rows
    tiles = up(lines, groups) // groups
    f32 = jnp.float32

    planes = 2 * frames

    def unpacked(block, plane, line):
        down, right = divmod(plane * rows + line, groups)
        return gathered_ref[place(block, slabs), down * coils : (down + 1) * coils, right * readout : (right + 1) * readout]

    if tiles * groups != lines:
        x_ref[...] = jnp.zeros_like(x_ref)
    for line in range(lines):
        block, inner = divmod(line, rows)
        group, tile = divmod(line, tiles)
        start = (LAGS + tile) * LANES + group * readout
        for plane in range(planes):
            x_ref[plane * coils : (plane + 1) * coils, start : start + readout] = unpacked(block, plane, inner)
    lane = lax.broadcasted_iota(jnp.int32, (2 * cell, LANES), 1)
    for back in range(1, LAGS + 1):
        source = (LAGS + tiles - back) * LANES
        wrapped = pltpu.roll(x_ref[:, source : source + LANES], readout, 1)
        target = (LAGS - back) * LANES
        x_ref[:, target : target + LANES] = jnp.where(lane >= readout, wrapped, 0.0)

    column = lane % readout
    inside = [(column + e - HALF >= 0) & (column + e - HALF < readout) for e in range(SPAN)]

    stacked = stacks(tiles)
    held = SPAN if stacked else 1

    def patches(tile):
        source = pl.ds(lane_tile(tile), LANES)
        if stacked:
            targets = [(lag, tile - LAGS + lag) for lag in range(SPAN) if 0 <= tile - LAGS + lag < tiles]
        else:
            targets = [(0, tile)]
        cells = x_ref[:, source]
        for e in range(SPAN):
            moved = cells if e == HALF else pltpu.roll(cells, (HALF - e) % LANES, 1)
            high, low = split(jnp.where(inside[e], moved, 0.0))
            for lag, target in targets:
                at = pl.ds(lane_tile(target), LANES)
                for part in range(2):
                    first = (2 * lag + part) * band + e * cell
                    z_ref[first : first + cell, at] = high[part * cell : (part + 1) * cell]
                    first += 2 * held * band
                    z_ref[first : first + cell, at] = low[part * cell : (part + 1) * cell]
            if stacked and tile >= LAGS:
                at = pl.ds(lane_tile(tile - LAGS), LANES)
                for part in range(2):
                    first = part * pad + e * cell
                    zc_ref[first : first + cell, at] = high[part * cell : (part + 1) * cell]
                    first += 2 * pad
                    zc_ref[first : first + cell, at] = low[part * cell : (part + 1) * cell]

    if stacked:
        for tile in range(LAGS + tiles):
            patches(tile)
    else:
        repeat(LAGS + tiles, patches)

    def centre(tile):
        source = pl.ds(lane_tile(tile + LAGS), LANES)
        at = pl.ds(lane_tile(tile), LANES)
        for piece in range(4):
            first = piece * pad
            if not stacked:
                zc_ref[first : first + band, at] = z_ref[piece * band : (piece + 1) * band, source]
            zc_ref[first + band : first + pad, at] = jnp.zeros((pad - band, LANES), jnp.bfloat16)

    repeat(tiles, centre)

    line_base = lane // readout * tiles
    acc_ref[...] = jnp.zeros_like(acc_ref)

    def energy(tile):
        cells = x_ref[:, pl.ds(lane_tile(tile + LAGS), LANES)]
        line = line_base + tile
        covers = jnp.minimum(line + HALF, lines - 1) - jnp.maximum(line - HALF, 0) + 1
        acc_ref[...] += cells * cells * covers.astype(f32)

    repeat(tiles, energy)
    row = lax.broadcasted_iota(jnp.int32, (2 * cell, LANES), 0)
    frame = row // coils % frames
    covers_t = jnp.minimum(frame + HALF, frames - 1) - jnp.maximum(frame - HALF, 0) + 1
    covers_x = jnp.minimum(column + HALF, readout - 1) - jnp.maximum(column - HALF, 0) + 1
    weighted = acc_ref[...] * (covers_t * covers_x).astype(f32)
    trace = jnp.sum(jnp.sum(weighted, axis=1, keepdims=True), axis=0, keepdims=True)
    scale = trace / (SPAN**3 * coils) + 1e-06

    def product(left, right):
        half = left.shape[0] // 2
        both = lax.dot_general(left, right[: 2 * pad], NT, preferred_element_type=f32)
        cross = lax.dot_general(left[:half], right[2 * pad :], NT, preferred_element_type=f32)
        return both[:half] + both[half:] + cross

    mrow = lax.broadcasted_iota(jnp.int32, (band, pad), 0) // coils % frames
    mcol = lax.broadcasted_iota(jnp.int32, (band, pad), 1) // coils % frames
    mixes = []
    for shift in range(-frames + 1, frames):
        mask = jnp.zeros((band, pad), f32)
        for i in range(frames):
            for j in range(frames):
                if 0 <= i + shift < frames and 0 <= j + shift < frames:
                    count = sum(
                        abs(i - t) <= HALF and abs(j - t) <= HALF and 0 <= t + shift < frames for t in range(frames)
                    )
                    mask = jnp.where((mrow == i) & (mcol == j), float(count), mask)
        mixes.append((shift, mask))

    def mixed(gram):
        total = None
        for shift, mask in mixes:
            moved = gram
            if shift:
                moved = pltpu.roll(pltpu.roll(gram, -shift * coils % pad, 1), -shift * coils % band, 0)
            total = moved * mask if total is None else total + moved * mask
        return total

    def complex_gram(sums):
        real = sums[:band, :pad] + sums[band:, pad:]
        imag = sums[:band, pad:] - sums[band:, :pad]
        return mixed(real), mixed(imag)

    slot = 0
    order = []

    def put(real, imag, lag, weight):
        nonlocal slot
        lhs_ref[:band, slot * pad : (slot + 1) * pad] = real
        lhs_ref[band:, slot * pad : (slot + 1) * pad] = imag
        order.append((lag, weight))
        slot += 1

    def put_both(pair, lag, weight, back_weight):
        real, imag = pair
        put(real, imag, lag, weight)
        fill = jnp.zeros((pad - band, pad), f32)
        real_t = jnp.transpose(jnp.concatenate([real, fill], axis=0))[:band]
        imag_t = jnp.transpose(jnp.concatenate([imag, fill], axis=0))[:band]
        put(real_t, -imag_t, -lag, back_weight)

    window = lax.broadcasted_iota(jnp.int32, (cell, up(width, LANES)), 1)
    my_line = me * rows + window // readout
    valid = [((my_line - b + HALF >= 0) & (my_line - b + HALF < lines)).astype(f32) for b in range(SPAN)]

    def lag_weight(lag):
        total = None
        for b in range(SPAN):
            if 0 <= b + lag < SPAN:
                total = valid[b] if total is None else total + valid[b]
        return total

    if stacked:
        every = product(z_ref[...], zc_ref[...])
    depth = max(d for d in range(1, 17) if tiles % d == 0)
    for lag in range(SPAN):

        def part(step):
            left = z_ref[:, pl.ds(lane_tile(LAGS - lag + step * depth), depth * LANES)]
            right = zc_ref[:, pl.ds(lane_tile(step * depth), depth * LANES)]
            return product(left, right)

        if stacked:
            sums = every[2 * band * lag : 2 * band * (lag + 1)]
        else:
            sums = lax.fori_loop(
                0, tiles // depth, lambda step, total: total + part(step), jnp.zeros((2 * band, 2 * pad), f32)
            )
        pair = complex_gram(sums)
        if lag == 0:
            put(*pair, 0, lag_weight(0))
        else:
            put_both(pair, lag, lag_weight(lag), lag_weight(-lag))

    def edge(first, second):
        group, tile = divmod(first, tiles)
        other = second % tiles
        start = tile * LANES if stacked else (LAGS + tile) * LANES
        here = lax.broadcasted_iota(jnp.int32, (2 * band, LANES), 1) // readout == group
        halves = []
        for base in (0, 2 * held * band):
            value = z_ref[base : base + 2 * band, start : start + LANES].astype(f32)
            halves.append(jnp.where(here, value, 0.0).astype(jnp.bfloat16))
        left = jnp.concatenate(halves, axis=0)
        return complex_gram(product(left, zc_ref[:, other * LANES : (other + 1) * LANES]))

    last = lines - 1
    put(*edge(last - 1, last - 1), 0, -valid[0])
    put(*edge(last, last), 0, -(valid[0] + valid[1]))
    put(*edge(0, 0), 0, -(valid[3] + valid[4]))
    put(*edge(1, 1), 0, -valid[4])
    put_both(edge(last - 1, last), 1, -valid[0], -valid[1])
    put_both(edge(0, 1), 1, -valid[3], -valid[4])

    reach = up(LAGS, rows) // rows
    for j in range(-reach, reach + 1):
        block = me + j
        exists = (block >= 0) & (block < slabs)
        block = jnp.clip(block, 0, slabs - 1)
        for line in range(rows):
            start = (j + reach) * width + line * readout
            for plane in range(planes):
                held = jnp.where(exists, unpacked(block, plane, line), 0.0)
                xw_ref[plane * coils : (plane + 1) * coils, start : start + readout] = held
    extent = xw_ref.shape[1]
    spread = lax.broadcasted_iota(jnp.int32, (2 * cell, extent), 1) % readout
    around = xw_ref[...]
    wide = up(width, LANES)
    for e in range(SPAN):
        moved = around if e == HALF else pltpu.roll(around, (HALF - e) % extent, 1)
        near = spread + e - HALF
        moved = jnp.where((near >= 0) & (near < readout), moved, 0.0)
        for lag in range(-LAGS, LAGS + 1):
            start = (reach * rows + lag) * readout
            piece = moved[:, start : start + wide]
            for index, (at, weight) in enumerate(order):
                if at == lag:
                    first = index * pad + e * cell
                    for part in range(2):
                        high, low = split(piece[part * cell : (part + 1) * cell] * weight)
                        rhs_ref[first : first + cell, part * wide : (part + 1) * wide] = high
                        rhs_ref[first : first + cell, (2 + part) * wide : (3 + part) * wide] = low
    for index in range(len(order)):
        first = index * pad
        rhs_ref[first + band : first + pad, :] = jnp.zeros((pad - band, 4 * wide), jnp.bfloat16)

    high, low = split(lhs_ref[...])
    lead = rhs_ref[:, : 2 * wide]
    total = lax.dot_general(high, lead, NN, preferred_element_type=f32)
    total += lax.dot_general(low, lead, NN, preferred_element_type=f32)
    total += lax.dot_general(high, rhs_ref[:, 2 * wide :], NN, preferred_element_type=f32)
    real = total[:band, :wide] + total[band:, wide:]
    imag = total[:band, wide:] - total[band:, :wide]

    factor = 1.0 / (SPAN**3 * scale)
    column = window % readout
    for part, values in enumerate((real, imag)):
        folded = jnp.zeros((cell, wide), f32)
        for e in range(SPAN):
            moved = values[e * cell : (e + 1) * cell]
            if e != HALF:
                moved = pltpu.roll(moved, (e - HALF) % wide, 1)
            near = column - e + HALF
            folded += jnp.where((near >= 0) & (near < readout), moved, 0.0)
        folded = folded * factor
        for line in range(rows):
            for f in range(frames):
                kept = measured_ref[part, :, line, f, :]
                at = (slice(f * coils, (f + 1) * coils), slice(line * readout, (line + 1) * readout))
                out_ref[part, :, line, f, :] = jnp.where(hit_ref[at] > 0, kept, folded[at])


def pack(lines_ref, estimate_ref, packed_ref, hit_ref):
    _, coils, rows, frames, readout = estimate_ref.shape
    shape = hit_ref.shape
    line = lax.axis_index("slab") * rows + lax.broadcasted_iota(jnp.int32, shape, 1) // readout
    frame = lax.broadcasted_iota(jnp.int32, shape, 0) // coils
    hit = jnp.zeros(shape, jnp.int32)
    for f in range(frames):
        for sample in range(lines_ref.shape[1]):
            hit = jnp.where((line == lines_ref[f, sample]) & (frame == f), 1, hit)
    hit_ref[...] = hit
    groups = LANES // readout
    for part in range(2):
        for f in range(frames):
            for line in range(rows):
                down, right = divmod((part * frames + f) * rows + line, groups)
                at = (0, slice(down * coils, (down + 1) * coils), slice(right * readout, (right + 1) * readout))
                packed_ref[at] = estimate_ref[part, :, line, f, :]
    packed = packed_ref[0]
    for copy in range(1, packed_ref.shape[0]):
        packed_ref[copy] = packed


def nearby(slabs):
    return 2 if slabs % 2 == 0 else 1


def place(block, slabs):
    near = nearby(slabs)
    return block % near * (slabs // near) + block // near


def gather(copies, slabs):
    near, far = nearby(slabs), slabs // nearby(slabs)
    alike = [[i + j * near for j in range(far)] for i in range(near)]
    chips = [[i * near + j for j in range(near)] for i in range(far)]
    half = lax.all_to_all(copies, "slab", 0, 0, axis_index_groups=alike)
    return lax.all_gather(half, "slab", axis_index_groups=chips, tiled=True)


def stacks(tiles):
    return tiles <= 16


def local(estimate, measured, sampled_lines):
    _, coils, frames, rows, readout = estimate.shape
    slabs = lax.axis_size("slab")
    cell = coils * frames
    width = rows * readout
    band = SPAN * cell
    pad = up(band, LANES)
    wide = up(width, LANES)
    groups = LANES // readout
    tiles = up(slabs * rows, groups) // groups
    reach = up(LAGS, rows) // rows
    slots = 2 * SPAN - 1 + 8
    columns = (tiles if stacks(tiles) else LAGS + tiles) * LANES

    vmem = pl.BlockSpec(memory_space=pltpu.VMEM)
    packed, hit = pl.pallas_call(
        pack,
        out_shape=(
            jax.ShapeDtypeStruct((slabs // nearby(slabs), up(2 * frames * rows, groups) // groups * coils, LANES), jnp.float32),
            jax.ShapeDtypeStruct((cell, wide), jnp.int32),
        ),
        in_specs=[pl.BlockSpec(memory_space=pltpu.SMEM), vmem],
        out_specs=(vmem, vmem),
        compiler_params=pltpu.CompilerParams(vmem_limit_bytes=56 * 1024 * 1024),
        name="pack",
    )(sampled_lines, jnp.swapaxes(estimate, 2, 3))
    gathered = gather(packed, slabs)
    sizes = (slabs, coils, frames, rows, readout)
    result = pl.pallas_call(
        functools.partial(kernel, sizes),
        out_shape=jax.ShapeDtypeStruct((2, coils, rows, frames, readout), jnp.float32),
        in_specs=[vmem, vmem, vmem],
        out_specs=vmem,
        scratch_shapes=[
            pltpu.VMEM((2 * cell, (LAGS + tiles) * LANES), jnp.float32),
            pltpu.VMEM((4 * band * (SPAN if stacks(tiles) else 1), columns), jnp.bfloat16),
            pltpu.VMEM((4 * pad, tiles * LANES), jnp.bfloat16),
            pltpu.VMEM((2 * cell, LANES), jnp.float32),
            pltpu.VMEM((2 * cell, up((2 * reach + 1) * width + LANES, LANES)), jnp.float32),
            pltpu.VMEM((2 * band, slots * pad), jnp.float32),
            pltpu.VMEM((slots * pad, 4 * wide), jnp.bfloat16),
        ],
        compiler_params=pltpu.CompilerParams(vmem_limit_bytes=40 * 1024 * 1024),
        name="filter_step",
    )(hit, gathered, jnp.swapaxes(measured, 2, 3))
    return jnp.swapaxes(result, 2, 3)


def solution(mesh):
    placed = (
        P(None, None, "grp", "slab", None),
        P(None, None, "grp", "slab", None),
        P("grp", None),
    )
    return jax.shard_map(
        local,
        mesh=mesh,
        in_specs=placed,
        out_specs=P(None, None, "grp", "slab", None),
        check_vma=False,
    )
```
